32 devices in a mesh: ctx: 16 (over z, y, core), fsdp: 2 (over x).
Axes of the slice: x: 2, y: 2, z: 4, core: 2. Of those that a mesh axis runs over, the one named last changes fastest.
Arguments:
- inputs: bfloat16 [2, 2048, 2048], P('fsdp', 'ctx'), may hold values from -6 to 6
- gain_attn: bfloat16 [2048], P(('ctx', 'fsdp')), may hold values from 0.5 to 1.5
- w_query: bfloat16 [2048, 2048], P(('ctx', 'fsdp')), may hold values from -0.125 to 0.125
- w_key: bfloat16 [2048, 512], P(('ctx', 'fsdp')), may hold values from -0.125 to 0.125
- w_value: bfloat16 [2048, 512], P(('ctx', 'fsdp')), may hold values from -0.125 to 0.125
- w_out: bfloat16 [2048, 2048], P(None, ('ctx', 'fsdp')), may hold values from -1.5 to 1.5
- gain_moe: bfloat16 [2048], P(('ctx', 'fsdp')), may hold values from 0.5 to 1.5
- w_router: bfloat16 [2048, 16], P(('ctx', 'fsdp')), may hold values from -0.0625 to 0.0625
- shared_gate: bfloat16 [2048, 2816], P(('ctx', 'fsdp')), may hold values from -0.125 to 0.125
- shared_up: bfloat16 [2048, 2816], P(('ctx', 'fsdp')), may hold values from -0.125 to 0.125
- shared_down: bfloat16 [2816, 2048], P(None, ('ctx', 'fsdp')), may hold values from -0.109375 to 0.109375
- expert_gate: bfloat16 [16, 2048, 1408], P('ctx', 'fsdp'), may hold values from -0.125 to 0.125
- expert_up: bfloat16 [16, 2048, 1408], P('ctx', 'fsdp'), may hold values from -0.125 to 0.125
- expert_down: bfloat16 [16, 1408, 2048], P('ctx', 'fsdp'), may hold values from -0.3125 to 0.3125
- positions: int32 [2, 2048], P('fsdp'), may hold values from 0 to 2047, as said below
- routes: int32 [2, 2048, 6], P('fsdp', 'ctx'), may hold values from 0 to 15, all different within a row; in each aligned block of 128 rows (0 to 127, 128 to 255, ..., all dimensions but the last counted through in order) at most 72 rows name the same one
- cotangent: bfloat16 [2, 2048, 2048], P('fsdp', 'ctx'), may hold values from -6 to 6
Outputs:
- output: bfloat16 [2, 2048, 2048], P('fsdp', 'ctx')
- grad_inputs: bfloat16 [2, 2048, 2048], P('fsdp', 'ctx')
- grad_gain_attn: float32 [2048], P(('ctx', 'fsdp'))
- grad_w_query: float32 [2048, 2048], P(('ctx', 'fsdp'))
- grad_w_key: float32 [2048, 512], P(('ctx', 'fsdp'))
- grad_w_value: float32 [2048, 512], P(('ctx', 'fsdp'))
- grad_w_out: float32 [2048, 2048], P(None, ('ctx', 'fsdp'))
- grad_gain_moe: float32 [2048], P(('ctx', 'fsdp'))
- grad_w_router: float32 [2048, 16], P(('ctx', 'fsdp'))
- grad_shared_gate: float32 [2048, 2816], P(('ctx', 'fsdp'))
- grad_shared_up: float32 [2048, 2816], P(('ctx', 'fsdp'))
- grad_shared_down: float32 [2816, 2048], P(None, ('ctx', 'fsdp'))
- grad_expert_gate: float32 [16, 2048, 1408], P('ctx', 'fsdp')
- grad_expert_up: float32 [16, 2048, 1408], P('ctx', 'fsdp')
- grad_expert_down: float32 [16, 1408, 2048], P('ctx', 'fsdp')
The draws below stay inside these ranges and needn't reach their ends.
Inputs may be any that keep to these rules, and one draw needn't show every extreme that they name: In each sequence the 128 stored rows of one ctx index hold position block p and then position block 31 - p, each of 64 consecutive positions in rising order; every p below 16 belongs to exactly one ctx index, which one is drawn from the seed. `routes`: each row names 6 different experts. Among the 128 rows of one device no expert is named more than 72 times, and in some device's rows an expert is named exactly 72 times.
All inputs are finite; a program needn't handle non-finite values.
Results may differ from the reference program's by a relative error of at most 0.019.
Values may be sent and summed in bfloat16 or wider, within the bound.
No kernel may reach another device: no remote copies, remote signals or barrier semaphores. Data moves between devices by JAX's collectives and lax.ppermute only.
A program may use at most 384 MiB of HBM per device.

```python
import math
import jax
import jax.numpy as jnp
import numpy as np
from jax import lax

D = 2048
HEADS = 16
KV_HEADS = 4
HEAD_DIM = 128
FF = 1408
TOP = 6
TOK_CTX = 128
EXPERTS = 16
SH_FF = 2816
LEN = 2048
NSEQ = 2
CAP = 72
N_CTX = 16


def draw_positions(key, part):
    key = jax.random.fold_in(key, 11)
    pair_count = LEN // TOK_CTX
    half_block = TOK_CTX // 2
    seq_keys = jax.random.split(key, NSEQ)

    def one_order(seq_key):
        return jax.random.permutation(seq_key, pair_count).astype(jnp.int32)
    orders = jax.vmap(one_order)(seq_keys)
    offsets = jnp.arange(half_block, dtype=jnp.int32)
    lower_block = orders[:, :, None] * half_block + offsets[None, None, :]
    upper_block = (2 * pair_count - 1 - orders)[:, :, None] * half_block + offsets[None, None, :]
    return jnp.concatenate([lower_block, upper_block], axis=2).reshape(NSEQ, LEN).astype(jnp.int32)


def block_levels(key, dims, cuts, smallest, high):
    level, own = 1.0, jax.random.fold_in(key, 6)
    for position, blocks in cuts:
        steps = jnp.exp(jax.random.uniform(jax.random.fold_in(own, position), (blocks,), jnp.float32, smallest / len(cuts), high / len(cuts)))
        level = level * jnp.repeat(steps, dims[position] // blocks).reshape([-1 if axis == position else 1 for axis in range(len(dims))])
    return level


def deal_out(rng, own, number, rows, number_of, top, most, slope):
    ranking = jax.random.permutation(rng, number_of)
    crowded, usual = shares(number_of, rows * top, most, slope, True), shares(number_of, rows * top, most, slope, False)
    places = jnp.arange(number_of)

    def named(lengths, offset_by):
        used = int((lengths > 0).sum())
        fixed = max(1, used // 4)
        shifted = fixed + (places - fixed + offset_by * (used - fixed)) % max(1, number_of - fixed)
        return jnp.zeros((number_of,), jnp.int32).at[ranking[jnp.where(places < fixed, places, shifted)]].set(jnp.asarray(lengths, jnp.int32))

    lengths = jnp.where(number % 4 == 0, named(crowded, number // 4), named(usual, number - number // 4 - 1))
    mixed = jax.random.permutation(jax.random.fold_in(own, 3), number_of)
    giver, taker = mixed[0:number_of // 2 * 2:2], mixed[1:number_of // 2 * 2:2]
    slack = jnp.minimum(lengths[giver] - 1, most - lengths[taker]) // 2
    slack = jnp.where((giver == ranking[0]) | (taker == ranking[0]) | (lengths[taker] == 0), 0, jnp.maximum(slack, 0))
    shifted = jax.random.randint(jax.random.fold_in(own, 4), (number_of // 2,), 0, 1 << 20) % (slack + 1)
    lengths = lengths.at[giver].add(-shifted).at[taker].add(shifted)
    members = jnp.searchsorted(jnp.cumsum(lengths), jnp.arange(rows * top), side="right").astype(jnp.int32)
    listing = members.reshape(top, rows).T
    listing = listing[jax.random.permutation(jax.random.fold_in(own, 1), rows)]
    offset_by = jax.random.randint(jax.random.fold_in(own, 2), (rows, 1), 0, top)
    return jnp.take_along_axis(listing, (jnp.arange(top)[None, :] + offset_by) % top, axis=1)


def shares(count, total, reach, skew, full):
    weights = [(1 << 20) // math.isqrt(rank ** skew) + 1 for rank in range(1, count + 1)]
    largest = reach if full else min(reach, max(-(-total // count), total * weights[0] // sum(weights)))
    least = 1 if total - largest >= count - 1 else 0
    counts, surplus = [largest] + [least] * (count - 1), total - largest - least * (count - 1)
    while surplus > 0:
        candidates = [i for i in range(1, count) if counts[i] < largest] or [i for i in range(1, count) if counts[i] < reach]
        whole, left = sum([weights[i] for i in candidates]), surplus
        for i in candidates:
            extra = min(reach - counts[i], max(1, left * weights[i] // whole), surplus)
            counts[i] = counts[i] + extra
            surplus = surplus - extra
    return np.array(counts)


def bell_draw(key, shape, width, bound, cuts=(), kind=jnp.bfloat16):
    level = block_levels(key, shape, cuts, -0.22, 0.18) if cuts else 1.0
    entries = jax.random.normal(key, shape, jnp.float32) * width * level
    return jnp.minimum(jnp.maximum(entries, -bound), bound).astype(kind)


def setup_inputs(seed: int = 0) -> dict:
    splits = jax.random.split(jax.random.key(seed), 18)
    inputs = bell_draw(splits[0], (NSEQ, LEN, D), 1.0, 6.0, ((0, 2), (1, 16)))
    gain_attn = jnp.clip(1.0 + 0.1 * jax.random.normal(splits[1], (D,), jnp.float32), 0.5, 1.5).astype(jnp.bfloat16)
    w_query = bell_draw(splits[2], (D, HEADS * HEAD_DIM), D ** -0.5, 0.125, ((0, 32),))
    w_key = bell_draw(splits[3], (D, KV_HEADS * HEAD_DIM), D ** -0.5, 0.125, ((0, 32),))
    w_value = bell_draw(splits[4], (D, KV_HEADS * HEAD_DIM), D ** -0.5, 0.125, ((0, 32),))
    w_out = bell_draw(splits[5], (HEADS * HEAD_DIM, D), (HEADS * HEAD_DIM * 16 // LEN) ** -0.5, 1.5, ((1, 32),))
    gain_moe = jnp.clip(1.0 + 0.1 * jax.random.normal(splits[6], (D,), jnp.float32), 0.5, 1.5).astype(jnp.bfloat16)
    w_router = bell_draw(splits[7], (D, EXPERTS), (4 * D) ** -0.5, 0.0625, ((0, 32),))
    shared_gate = bell_draw(splits[8], (D, SH_FF), D ** -0.5, 0.125, ((0, 32),))
    shared_up = bell_draw(splits[9], (D, SH_FF), D ** -0.5, 0.125, ((0, 32),))
    shared_down = bell_draw(splits[10], (SH_FF, D), SH_FF ** -0.5, 0.109375, ((1, 32),))
    expert_gate = bell_draw(splits[11], (EXPERTS, D, FF), D ** -0.5, 0.125, ((0, 16), (1, 2)))
    expert_up = bell_draw(splits[12], (EXPERTS, D, FF), D ** -0.5, 0.125, ((0, 16), (1, 2)))
    expert_down = bell_draw(splits[13], (EXPERTS, FF, D), (FF // 4) ** -0.5, 0.3125, ((0, 16), (1, 2)))
    positions = draw_positions(jax.random.fold_in(splits[17], 71), 0)
    routes_keys = jax.random.split(jax.random.fold_in(splits[15], 1), NSEQ * LEN // TOK_CTX)
    routes_turns = jax.random.permutation(jax.random.fold_in(splits[15], 3), NSEQ * LEN // TOK_CTX)
    routes = jax.vmap(lambda own, number: deal_out(jax.random.fold_in(splits[15], 2), own, number, TOK_CTX, EXPERTS, TOP, CAP, 1))(routes_keys, routes_turns).reshape((NSEQ, LEN, TOP))
    cotangent = bell_draw(splits[16], (NSEQ, LEN, D), 1.0, 6.0, ((0, 2), (1, 16)))
    return {"inputs": inputs, "gain_attn": gain_attn, "w_query": w_query, "w_key": w_key, "w_value": w_value, "w_out": w_out, "gain_moe": gain_moe, "w_router": w_router, "shared_gate": shared_gate, "shared_up": shared_up, "shared_down": shared_down, "expert_gate": expert_gate, "expert_up": expert_up, "expert_down": expert_down, "positions": positions, "routes": routes, "cotangent": cotangent}


epsilon = 1e-06
rope_base = 600000.0
highest = lax.Precision.HIGHEST

@jax.custom_vjp
def low(v):
    return lax.optimization_barrier(v.astype(jnp.bfloat16)).astype(jnp.float32)

@jax.custom_vjp
def low_back(v):
    return v

def low_keep(v):
    return (low(v), None)

def low_pass(kept, grad):
    return (grad,)

def back_keep(v):
    return (v, None)

def back_low(kept, grad):
    return (low(grad),)
low.defvjp(low_keep, low_pass)
low_back.defvjp(back_keep, back_low)

def product(left, right):
    return jnp.dot(left, right, precision=highest, preferred_element_type=jnp.float32)

def rms_norm(values, gain):
    inverse = lax.rsqrt(lax.optimization_barrier(jnp.mean(values * values, axis=-1, keepdims=True)) + epsilon)
    return values * inverse * gain

def silu(values):
    return values * lax.logistic(values)

def rope_tables(position_row, head_size):
    half_size = head_size // 2
    freq_steps = jnp.arange(half_size, dtype=jnp.float32)
    frequency = rope_base ** (-(freq_steps / half_size))
    angles = position_row.astype(jnp.float32)[:, None] * frequency[None, :]
    return (jnp.cos(angles), jnp.sin(angles))

def rotate(values, cosine, sine_table):
    half_size = values.shape[-1] // 2
    first_half = values[..., :half_size]
    second_half = values[..., half_size:]
    cosine_wide = cosine[:, None, :]
    sine_wide = sine_table[:, None, :]
    return jnp.concatenate([first_half * cosine_wide - second_half * sine_wide, second_half * cosine_wide + first_half * sine_wide], axis=-1)

def attend(pieces):
    query, keys, values, seq_pos = pieces
    group = HEADS // KV_HEADS
    query_grouped = query.reshape(LEN, KV_HEADS, group, HEAD_DIM)
    scores = jnp.einsum('qkgd,skd->kgqs', query_grouped, keys, precision=highest) * HEAD_DIM ** (-0.5)
    scores = low_back(scores)
    allowed = seq_pos[:, None] >= seq_pos[None, :]
    scores = jnp.where(allowed[None, None], scores, -1e+30)
    peak = lax.optimization_barrier(jnp.max(scores, axis=-1, keepdims=True))
    raised = jnp.exp(scores - peak)
    probs = raised / lax.optimization_barrier(jnp.sum(raised, axis=-1, keepdims=True))
    mixed = jnp.einsum('kgqs,skd->qkgd', low(probs), values, precision=highest)
    return mixed.reshape(LEN, HEADS * HEAD_DIM)

def slot_tables(routes):
    block_count = NSEQ * N_CTX
    per_block = routes.reshape(block_count, TOK_CTX, TOP).astype(jnp.int32)
    named = jnp.any(per_block[..., None] == jnp.arange(EXPERTS, dtype=jnp.int32), axis=2).astype(jnp.int32)
    before = (jnp.cumsum(named, axis=1) - named).astype(jnp.int32)
    slot = jnp.take_along_axis(before, per_block, axis=2).astype(jnp.int32)
    block_ids = jnp.arange(block_count, dtype=jnp.int32)[:, None, None]
    token_ids = block_ids * TOK_CTX + jnp.arange(TOK_CTX, dtype=jnp.int32)[None, :, None] + jnp.zeros_like(per_block)
    pick_ids = token_ids * TOP + jnp.arange(TOP, dtype=jnp.int32)[None, None, :]
    target = (per_block * (block_count * CAP) + block_ids * CAP + slot).reshape(-1).astype(jnp.int32)
    total_slots = EXPERTS * block_count * CAP
    token_slot = jnp.zeros((total_slots,), jnp.int32).at[target].set(token_ids.reshape(-1).astype(jnp.int32))
    pick_slot = jnp.zeros((total_slots,), jnp.int32).at[target].set(pick_ids.reshape(-1).astype(jnp.int32))
    live_slot = jnp.zeros((total_slots,), jnp.float32).at[target].set(1.0)
    shape_out = (EXPERTS, block_count * CAP)
    return (token_slot.reshape(shape_out), pick_slot.reshape(shape_out), live_slot.reshape(shape_out))

def reference(inputs, gain_attn, w_query, w_key, w_value, w_out, gain_moe, w_router, shared_gate, shared_up, shared_down, expert_gate, expert_up, expert_down, positions, routes, cotangent):
    token_count = NSEQ * LEN
    token_slot, pick_slot, live_slot = slot_tables(routes)
    flat_routes = routes.reshape(token_count, TOP).astype(jnp.int32)
    cosine, sine_table = rope_tables(positions.reshape(-1), HEAD_DIM)

    def layer(layer_in, gain_one, query_weight, key_weight, value_weight, out_weight, gain_two, router_weight, share_gate, share_up, share_down, routed_gate, routed_up, routed_down):
        flat_in = layer_in.reshape(token_count, D)
        attn_in = low(rms_norm(flat_in, gain_one))
        query = low_back(product(attn_in, query_weight)).reshape(token_count, HEADS, HEAD_DIM)
        keys = low_back(product(attn_in, key_weight)).reshape(token_count, KV_HEADS, HEAD_DIM)
        values = low(low_back(product(attn_in, value_weight))).reshape(NSEQ, LEN, KV_HEADS, HEAD_DIM)
        query = low(rotate(query, cosine, sine_table)).reshape(NSEQ, LEN, HEADS, HEAD_DIM)
        keys = low(rotate(keys, cosine, sine_table)).reshape(NSEQ, LEN, KV_HEADS, HEAD_DIM)
        mixed = lax.map(jax.checkpoint(attend), (query, keys, values, positions))
        attended = low(low_back(mixed.reshape(token_count, HEADS * HEAD_DIM)))
        state = flat_in + low_back(product(attended, out_weight))
        moe_in = low(rms_norm(state, gain_two))
        logits = product(moe_in, router_weight)
        chosen = jnp.take_along_axis(logits, flat_routes, axis=1)
        peak = lax.optimization_barrier(jnp.max(chosen, axis=1, keepdims=True))
        raised = jnp.exp(chosen - peak)
        gates = raised / lax.optimization_barrier(jnp.sum(raised, axis=1, keepdims=True))
        shared_a = low_back(product(moe_in, share_gate))
        shared_b = low_back(product(moe_in, share_up))
        shared_out = product(low(silu(shared_a) * shared_b), share_down)
        gate_flat = gates.reshape(-1)

        def expert_pass(total, pieces):
            gate_w, up_w, down_w, token_idx, pick_idx, live = pieces
            picked_rows = low_back(moe_in[token_idx])
            expert_a = low_back(product(picked_rows, gate_w))
            expert_b = low_back(product(picked_rows, up_w))
            expert_hidden = low(silu(expert_a) * expert_b)
            expert_out = low(low_back(product(expert_hidden, down_w)))
            weight = live * gate_flat[pick_idx]
            return (total.at[token_idx].add(weight[:, None] * expert_out), None)
        routed, unused = lax.scan(jax.checkpoint(expert_pass), jnp.zeros((token_count, D), jnp.float32), (routed_gate, routed_up, routed_down, token_slot, pick_slot, live_slot))
        return (state + routed + shared_out).reshape(NSEQ, LEN, D)
    output, pullback = jax.vjp(layer, inputs.astype(jnp.float32), gain_attn.astype(jnp.float32), w_query.astype(jnp.float32), w_key.astype(jnp.float32), w_value.astype(jnp.float32), w_out.astype(jnp.float32), gain_moe.astype(jnp.float32), w_router.astype(jnp.float32), shared_gate.astype(jnp.float32), shared_up.astype(jnp.float32), shared_down.astype(jnp.float32), expert_gate.astype(jnp.float32), expert_up.astype(jnp.float32), expert_down.astype(jnp.float32))
    grads = pullback(cotangent.astype(jnp.float32))
    return (output.astype(jnp.bfloat16), grads[0].astype(jnp.bfloat16), grads[1], grads[2], grads[3], grads[4], grads[5], grads[6], grads[7], grads[8], grads[9], grads[10], grads[11], grads[12], grads[13])
```

```python
import jax
import jax.numpy as jnp
from jax import lax
from jax.sharding import PartitionSpec as P

HEADS = 16
KV_HEADS = 4
HEAD_DIM = 128
TOP = 6


epsilon = 1e-06
rope_base = 600000.0
highest = lax.Precision.HIGHEST


def rope_tables(position_row, head_size):
    half_size = head_size // 2
    freq_steps = jnp.arange(half_size, dtype=jnp.float32)
    frequency = rope_base ** (-(freq_steps / half_size))
    angles = position_row.astype(jnp.float32)[:, None] * frequency[None, :]
    return (jnp.cos(angles), jnp.sin(angles))


def rotate(values, cosine, sine_table):
    half_size = values.shape[-1] // 2
    first_half = values[..., :half_size]
    second_half = values[..., half_size:]
    cosine_wide = cosine[:, None, :]
    sine_wide = sine_table[:, None, :]
    return jnp.concatenate(
        [
            first_half * cosine_wide - second_half * sine_wide,
            second_half * cosine_wide + first_half * sine_wide,
        ],
        axis=-1,
    )


def silu_slope(values):
    sigmoid_part = lax.logistic(values)
    return sigmoid_part * (1.0 + values * (1.0 - sigmoid_part))


def norm_back(grad_normed, normed, inverse, gain):
    grad_gain = jnp.sum(grad_normed * normed, axis=0)
    scaled = grad_normed * gain
    grad_values = inverse * (scaled - normed * jnp.mean(scaled * normed, axis=-1, keepdims=True))
    return (grad_gain, grad_values)


CORES = 2
LINES = 2


def ctx_place():
    here = lax.axis_index("ctx")
    return here // (CORES * LINES), here // CORES % LINES, here % CORES


def shift_pairs(step):
    count = lax.axis_size("ctx")
    planes = count // (CORES * LINES)
    return [
        (i, (i // (CORES * LINES) + step) % planes * (CORES * LINES) + i % (CORES * LINES))
        for i in range(count)
    ]


def flip_pairs(bit):
    return [(i, i ^ bit) for i in range(lax.axis_size("ctx"))]


def plane_order():
    planes = lax.axis_size("ctx") // (CORES * LINES)
    return sorted(range(1, planes), key=lambda k: (min(k, planes - k), k))


def relative_blocks():
    planes = lax.axis_size("ctx") // (CORES * LINES)
    z, y, c = ctx_place()
    k, j, i = jnp.meshgrid(jnp.arange(planes), jnp.arange(LINES), jnp.arange(CORES), indexing="ij")
    return (((z - k) % planes) * (CORES * LINES) + (y ^ j) * CORES + (c ^ i)).reshape(-1)


def absolute_blocks():
    planes = lax.axis_size("ctx") // (CORES * LINES)
    z, y, c = ctx_place()
    b = jnp.arange(lax.axis_size("ctx"))
    bz, by, bc = b // (CORES * LINES), b // CORES % LINES, b % CORES
    return ((z - bz) % planes) * (CORES * LINES) + (y ^ by) * CORES + (c ^ bc)


def gather_ctx(block):
    planes = lax.axis_size("ctx") // (CORES * LINES)
    found = {(0, 0, 0): block}
    for k in plane_order():
        found[k, 0, 0] = lax.ppermute(block, "ctx", shift_pairs(k))
    for k in [0] + plane_order():
        found[k, 1, 0] = lax.ppermute(found[k, 0, 0], "ctx", flip_pairs(CORES))
        for j in range(LINES):
            found[k, j, 1] = lax.ppermute(found[k, j, 0], "ctx", flip_pairs(1))
    return jnp.concatenate(
        [found[k, j, i] for k in range(planes) for j in range(LINES) for i in range(CORES)], axis=0
    )


def scatter_ctx(partial):
    planes = lax.axis_size("ctx") // (CORES * LINES)
    rows = partial.shape[0] // (planes * LINES * CORES)
    partial = partial.reshape(planes, LINES, CORES, rows, partial.shape[1])
    total = None
    for k in plane_order()[::-1] + [0]:
        sibling = lax.ppermute(partial[k, :, 1], "ctx", flip_pairs(1))
        chip = (partial[k, :, 0].astype(jnp.float32) + sibling.astype(jnp.float32)).astype(jnp.bfloat16)
        across = lax.ppermute(chip[1], "ctx", flip_pairs(CORES))
        line = chip[0].astype(jnp.float32) + across.astype(jnp.float32)
        if k:
            line = lax.ppermute(line.astype(jnp.bfloat16), "ctx", shift_pairs(-k)).astype(jnp.float32)
        total = line if total is None else total + line
    return total


def swap(block):
    return lax.ppermute(block, "fsdp", [(0, 1), (1, 0)])


def gather_fsdp(block, axis):
    if lax.axis_size("fsdp") != 2:
        return lax.all_gather(block, "fsdp", axis=axis, tiled=True)
    peer = swap(block)
    first = lax.axis_index("fsdp") == 0
    return jnp.concatenate(
        [jnp.where(first, block, peer), jnp.where(first, peer, block)], axis=axis
    )


def scatter_fsdp(total, axis):
    if lax.axis_size("fsdp") != 2:
        return lax.psum_scatter(
            total.astype(jnp.bfloat16), "fsdp", scatter_dimension=axis, tiled=True
        ).astype(jnp.float32)
    here = lax.axis_index("fsdp")
    half = total.shape[axis] // 2
    away = lax.dynamic_slice_in_dim(total, (1 - here) * half, half, axis)
    kept = lax.dynamic_slice_in_dim(total, here * half, half, axis)
    return kept + swap(away.astype(jnp.bfloat16)).astype(jnp.float32)


def spread(slices):
    rows, count, size = slices.shape
    moved = lax.all_to_all(
        slices.transpose(1, 0, 2), "ctx", split_axis=0, concat_axis=0, tiled=True
    )
    joined = gather_fsdp(moved, 1)
    return joined.reshape(-1, size)


def collect(grad, wide=False):
    count = lax.axis_size("ctx")
    grad = grad.reshape(count, grad.shape[0] // count, grad.shape[1])
    own = scatter_fsdp(grad, 1)
    if not wide:
        own = own.astype(jnp.bfloat16)
    moved = lax.all_to_all(own, "ctx", split_axis=0, concat_axis=0, tiled=True)
    return moved.astype(jnp.float32).transpose(1, 0, 2)


def dot32(spec, left, right):
    return jnp.einsum(spec, left, right, preferred_element_type=jnp.float32)


def body(
    inputs,
    gain_attn,
    w_query,
    w_key,
    w_value,
    w_out,
    gain_moe,
    w_router,
    shared_gate,
    shared_up,
    shared_down,
    expert_gate,
    expert_up,
    expert_down,
    positions,
    routes,
    cotangent,
):
    ctx_count = lax.axis_size("ctx")
    here = lax.axis_index("ctx")
    tok_rows = inputs.shape[1]
    width = inputs.shape[2]
    group = HEADS // KV_HEADS
    scale = HEAD_DIM ** (-0.5)
    experts = w_router.shape[1]
    length = tok_rows * ctx_count
    part_rows = w_query.shape[0]
    capacity = min(tok_rows, 3 * tok_rows * TOP // (2 * experts))
    low = jnp.bfloat16

    all_in = gather_ctx(inputs[0])
    small = jnp.concatenate(
        [w_router, gain_attn[:, None], gain_moe[:, None]], axis=1
    )
    small = jnp.pad(small, ((0, 0), (0, 128 - small.shape[1])))
    small = lax.all_gather(small, ("ctx", "fsdp"), axis=0, tiled=True)
    router_weight = small[:, :experts]
    gain_one = small[:, experts].astype(jnp.float32)
    gain_two = small[:, experts + 1].astype(jnp.float32)

    def head_slices(weight):
        return weight.reshape(part_rows, HEADS, HEAD_DIM)

    def kv_slices(weight):
        return jnp.repeat(weight.reshape(part_rows, KV_HEADS, HEAD_DIM), group, axis=1)

    attn_weight = spread(
        jnp.concatenate(
            [head_slices(w_query), kv_slices(w_key), kv_slices(w_value), head_slices(w_out.T)],
            axis=2,
        )
    )
    qkv_weight = attn_weight[:, : 3 * HEAD_DIM]
    out_weight = attn_weight[:, 3 * HEAD_DIM :]
    routed_gate = gather_fsdp(expert_gate, 1)[0]
    routed_up = gather_fsdp(expert_up, 1)[0]
    hidden_part = shared_gate.shape[1] // ctx_count
    shared_weight = spread(
        jnp.concatenate(
            [
                shared_gate.reshape(part_rows, ctx_count, hidden_part),
                shared_up.reshape(part_rows, ctx_count, hidden_part),
                shared_down.T.reshape(part_rows, ctx_count, hidden_part),
            ],
            axis=2,
        )
    )
    share_in = shared_weight[:, : 2 * hidden_part]
    share_down = shared_weight[:, 2 * hidden_part :]
    routed_down = gather_fsdp(expert_down, 1)[0]
    all_cot = gather_ctx(cotangent[0])
    order = relative_blocks()
    seq_pos = positions[0].reshape(ctx_count, tok_rows)[order].reshape(length)
    all_routes = lax.all_gather(routes[0].T, "ctx", axis=0, tiled=False)[order]

    wide_in = all_in.astype(jnp.float32)
    inverse_one = lax.rsqrt(jnp.mean(wide_in * wide_in, axis=-1, keepdims=True) + epsilon)
    attn_in = (wide_in * inverse_one * gain_one).astype(low)
    cosine, sine_table = rope_tables(seq_pos, HEAD_DIM)
    qkv = dot32("td,dh->th", attn_in, qkv_weight)
    query = rotate(qkv[:, None, :HEAD_DIM], cosine, sine_table)[:, 0].astype(low)
    keys = rotate(qkv[:, None, HEAD_DIM : 2 * HEAD_DIM], cosine, sine_table)[:, 0].astype(low)
    values = qkv[:, 2 * HEAD_DIM :].astype(low)
    scores = dot32("qd,sd->qs", query, keys) * scale
    scores = jnp.where(seq_pos[:, None] >= seq_pos[None, :], scores, -1e30)
    raised = jnp.exp(scores - jnp.max(scores, axis=-1, keepdims=True))
    probs = (raised / jnp.sum(raised, axis=-1, keepdims=True)).astype(low)
    attended = dot32("qs,sd->qd", probs, values).astype(low)
    state_part = dot32("th,dh->td", attended, out_weight).astype(low)
    token_in = inputs[0].astype(jnp.float32)
    state = token_in + scatter_ctx(state_part)

    inverse_two = lax.rsqrt(jnp.mean(state * state, axis=-1, keepdims=True) + epsilon)
    normed_two = state * inverse_two
    moe_in = (normed_two * gain_two).astype(low)
    all_moe = gather_ctx(moe_in)

    logits = dot32("td,de->et", all_moe, router_weight).reshape(experts, ctx_count, tok_rows)
    expert_ids = jnp.arange(experts, dtype=jnp.int32)
    named = jnp.any(all_routes[None] == expert_ids[:, None, None, None], axis=2)
    peak = jnp.max(jnp.where(named, logits, -1e30), axis=0, keepdims=True)
    chosen = jnp.where(named, jnp.exp(jnp.where(named, logits - peak, 0.0)), 0.0)
    gates = chosen / jnp.sum(chosen, axis=0, keepdims=True)

    mine = jnp.any(all_routes == here, axis=1)
    mine_count = mine.astype(jnp.int32)
    slot = jnp.cumsum(mine_count, axis=1) - mine_count
    placer = (
        (slot[:, None, :] == jnp.arange(capacity, dtype=jnp.int32)[None, :, None])
        & mine[:, None, :]
    )
    place = placer.astype(low)
    own_gate = jnp.sum(jnp.where(expert_ids[:, None, None] == here, gates, 0.0), axis=0)
    slot_gate = jnp.sum(jnp.where(placer, own_gate[:, None, :], 0.0), axis=2).reshape(-1, 1)

    def pick(rows):
        found = dot32("bst,btd->bsd", place, rows.reshape(ctx_count, tok_rows, width))
        return found.astype(low).reshape(ctx_count * capacity, width)

    def put(rows):
        return dot32("bst,bsd->btd", place, rows.reshape(ctx_count, capacity, width)).reshape(
            length, width
        )

    received = pick(all_moe)
    slot_cot = pick(all_cot)
    slot_grad = (slot_gate * slot_cot.astype(jnp.float32)).astype(low)
    expert_a = dot32("sd,df->sf", received, routed_gate)
    expert_b = dot32("sd,df->sf", received, routed_up)
    expert_act = expert_a * lax.logistic(expert_a)
    expert_hidden = (expert_act * expert_b).astype(low)
    grad_routed_down = dot32("sf,sd->fd", expert_hidden, slot_grad)
    grad_expert_down = scatter_fsdp(grad_routed_down, 0)[None]
    grad_hidden = dot32("sd,fd->sf", slot_grad, routed_down)
    grad_expert_a = (grad_hidden * expert_b * silu_slope(expert_a)).astype(low)
    grad_expert_b = (grad_hidden * expert_act).astype(low)
    row_grad = (
        dot32("sf,df->sd", grad_expert_a, routed_gate) + dot32("sf,df->sd", grad_expert_b, routed_up)
    ).astype(low)
    grad_expert_gate = scatter_fsdp(dot32("sd,sf->df", received, grad_expert_a), 0)[None]
    grad_expert_up = scatter_fsdp(dot32("sd,sf->df", received, grad_expert_b), 0)[None]

    shared_ab = dot32("td,df->tf", all_moe, share_in)
    shared_a, shared_b = shared_ab[:, :hidden_part], shared_ab[:, hidden_part:]
    shared_act = shared_a * lax.logistic(shared_a)
    shared_hidden = (shared_act * shared_b).astype(low)
    grad_shared_hidden = dot32("td,df->tf", all_cot, share_down)
    grad_shared_a = (grad_shared_hidden * shared_b * silu_slope(shared_a)).astype(low)
    grad_shared_b = (grad_shared_hidden * shared_act).astype(low)
    grad_shared_ab = jnp.concatenate([grad_shared_a, grad_shared_b], axis=1)
    moe_part = put(row_grad) + dot32("tf,df->td", grad_shared_ab, share_in)
    grad_moe_sum = scatter_ctx(moe_part.astype(low))

    expert_out = dot32("sf,fd->sd", expert_hidden, routed_down).astype(low).astype(jnp.float32)
    slot_score = jnp.sum(slot_cot.astype(jnp.float32) * expert_out, axis=1)
    score_blocks = jnp.sum(
        jnp.where(placer, slot_score.reshape(ctx_count, capacity, 1), 0.0), axis=1
    )
    grad_gates = lax.all_to_all(
        score_blocks[absolute_blocks()], "ctx", split_axis=0, concat_axis=0, tiled=True
    )
    out_part = put((slot_gate * expert_out).astype(low)) + dot32("tf,df->td", shared_hidden, share_down)
    output = (state + scatter_ctx(out_part.astype(low))).astype(low)

    home_gates = gates[:, 0]
    gate_mean = jnp.sum(home_gates * grad_gates, axis=0, keepdims=True)
    grad_logits = home_gates * (grad_gates - gate_mean)
    grad_router = jnp.einsum(
        "td,et->de", moe_in.astype(jnp.float32), grad_logits, precision=highest
    )
    grad_moe_in = grad_moe_sum + jnp.einsum(
        "et,de->td", grad_logits, router_weight.astype(jnp.float32), precision=highest
    )
    grad_gain_two, grad_through = norm_back(grad_moe_in, normed_two, inverse_two, gain_two)
    grad_state = cotangent[0].astype(jnp.float32) + grad_through
    all_proj = gather_ctx(grad_state.astype(low))

    grad_shared = jnp.concatenate(
        [
            dot32("td,tf->df", all_moe, grad_shared_ab),
            dot32("td,tf->df", all_cot, shared_hidden),
        ],
        axis=1,
    )
    shared_back = collect(grad_shared)
    narrow = collect(jnp.concatenate([grad_router, grad_gain_two[:, None]], axis=1), wide=True)
    narrow = jnp.sum(narrow, axis=1)

    grad_attended = dot32("td,dh->th", all_proj, out_weight).astype(low)
    grad_out_weight = dot32("td,th->dh", all_proj, attended)
    grad_probs = dot32("qd,sd->qs", grad_attended, values)
    wide_probs = probs.astype(jnp.float32)
    row_dot = jnp.sum(wide_probs * grad_probs, axis=-1, keepdims=True)
    grad_scores = (wide_probs * (grad_probs - row_dot)).astype(low)
    grad_query_rot = dot32("qs,sd->qd", grad_scores, keys) * scale
    grad_keys_rot = dot32("qs,qd->sd", grad_scores, query) * scale
    grad_values = dot32("qs,qd->sd", probs, grad_attended)
    grad_qkv = jnp.concatenate(
        [
            rotate(grad_query_rot[:, None], cosine, -sine_table)[:, 0].astype(low),
            rotate(grad_keys_rot[:, None], cosine, -sine_table)[:, 0].astype(low),
            grad_values.astype(low),
        ],
        axis=1,
    )
    attn_part = dot32("th,dh->td", grad_qkv, qkv_weight)
    grad_attn_in = scatter_ctx(attn_part.astype(low))
    grad_attn = jnp.concatenate([dot32("td,th->dh", attn_in, grad_qkv), grad_out_weight], axis=1)
    attn_back = collect(grad_attn)
    home_inverse = lax.rsqrt(jnp.mean(token_in * token_in, axis=-1, keepdims=True) + epsilon)
    grad_gain_one, grad_first = norm_back(
        grad_attn_in, token_in * home_inverse, home_inverse, gain_one
    )
    grad_inputs = (grad_state + grad_first).astype(low)
    grad_gain_attn = jnp.sum(collect(grad_gain_one[:, None], wide=True), axis=1)[:, 0]

    def kv_sum(grad):
        return jnp.sum(grad.reshape(part_rows, KV_HEADS, group, HEAD_DIM), axis=2).reshape(
            part_rows, KV_HEADS * HEAD_DIM
        )

    grad_w_query = attn_back[:, :, :HEAD_DIM].reshape(part_rows, -1)
    grad_w_key = kv_sum(attn_back[:, :, HEAD_DIM : 2 * HEAD_DIM])
    grad_w_value = kv_sum(attn_back[:, :, 2 * HEAD_DIM : 3 * HEAD_DIM])
    grad_w_out = attn_back[:, :, 3 * HEAD_DIM :].reshape(part_rows, -1).T
    return (
        output[None],
        grad_inputs[None],
        grad_gain_attn,
        grad_w_query,
        grad_w_key,
        grad_w_value,
        grad_w_out,
        narrow[:, experts],
        narrow[:, :experts],
        shared_back[:, :, :hidden_part].reshape(part_rows, -1),
        shared_back[:, :, hidden_part : 2 * hidden_part].reshape(part_rows, -1),
        shared_back[:, :, 2 * hidden_part :].reshape(part_rows, -1).T,
        grad_expert_gate,
        grad_expert_up,
        grad_expert_down,
    )


def solution(mesh):
    in_specs = (
        P("fsdp", "ctx", None),
        P(("ctx", "fsdp")),
        P(("ctx", "fsdp"), None),
        P(("ctx", "fsdp"), None),
        P(("ctx", "fsdp"), None),
        P(None, ("ctx", "fsdp")),
        P(("ctx", "fsdp")),
        P(("ctx", "fsdp"), None),
        P(("ctx", "fsdp"), None),
        P(("ctx", "fsdp"), None),
        P(None, ("ctx", "fsdp")),
        P("ctx", "fsdp", None),
        P("ctx", "fsdp", None),
        P("ctx", "fsdp", None),
        P("fsdp", None),
        P("fsdp", "ctx", None),
        P("fsdp", "ctx", None),
    )
    out_specs = (
        P("fsdp", "ctx", None),
        P("fsdp", "ctx", None),
        P(("ctx", "fsdp")),
        P(("ctx", "fsdp"), None),
        P(("ctx", "fsdp"), None),
        P(("ctx", "fsdp"), None),
        P(None, ("ctx", "fsdp")),
        P(("ctx", "fsdp")),
        P(("ctx", "fsdp"), None),
        P(("ctx", "fsdp"), None),
        P(("ctx", "fsdp"), None),
        P(None, ("ctx", "fsdp")),
        P("ctx", "fsdp", None),
        P("ctx", "fsdp", None),
        P("ctx", "fsdp", None),
    )
    return jax.shard_map(body, mesh=mesh, in_specs=in_specs, out_specs=out_specs, check_vma=False)
```

```python
import jax
import jax.numpy as jnp
from jax import lax
from jax.experimental import pallas as pl
from jax.experimental.pallas import tpu as pltpu
from jax.sharding import PartitionSpec as P

HEADS = 16
KV_HEADS = 4
HEAD_DIM = 128
TOP = 6


epsilon = 1e-06
rope_base = 600000.0
highest = lax.Precision.HIGHEST


def rope_tables(position_row, head_size):
    half_size = head_size // 2
    freq_steps = jnp.arange(half_size, dtype=jnp.float32)
    frequency = rope_base ** (-(freq_steps / half_size))
    angles = position_row.astype(jnp.float32)[:, None] * frequency[None, :]
    return (jnp.cos(angles), jnp.sin(angles))


def rotate(values, cosine, sine_table):
    half_size = values.shape[-1] // 2
    first_half = values[..., :half_size]
    second_half = values[..., half_size:]
    cosine_wide = cosine[:, None, :]
    sine_wide = sine_table[:, None, :]
    return jnp.concatenate(
        [
            first_half * cosine_wide - second_half * sine_wide,
            second_half * cosine_wide + first_half * sine_wide,
        ],
        axis=-1,
    )


def silu_slope(values):
    sigmoid_part = lax.logistic(values)
    return sigmoid_part * (1.0 + values * (1.0 - sigmoid_part))


def norm_back(grad_normed, normed, inverse, gain):
    grad_gain = jnp.sum(grad_normed * normed, axis=0)
    scaled = grad_normed * gain
    grad_values = inverse * (scaled - normed * jnp.mean(scaled * normed, axis=-1, keepdims=True))
    return (grad_gain, grad_values)


CORES = 2
LINES = 2
CHIP = CORES * LINES


def ctx_place():
    here = lax.axis_index("ctx")
    return here // CHIP, here // CORES % LINES, here % CORES


def plane_count():
    return lax.axis_size("ctx") // CHIP


def plane_order():
    planes = plane_count()
    return sorted(range(1, planes), key=lambda k: (min(k, planes - k), k))


def shift(values, step):
    planes = plane_count()
    pairs = [
        (i, (i // CHIP + step) % planes * CHIP + i % CHIP) for i in range(lax.axis_size("ctx"))
    ]
    return lax.ppermute(values, "ctx", pairs)


def flip(values, bit):
    return lax.ppermute(values, "ctx", [(i, i ^ bit) for i in range(lax.axis_size("ctx"))])


def swap(values):
    return lax.ppermute(values, "fsdp", [(0, 1), (1, 0)])


def part(values, index, axis=0):
    return lax.dynamic_index_in_dim(values, index, axis, keepdims=False)


def pair(mine, other, place, axis):
    first = place == 0
    return jnp.stack(
        [jnp.where(first, mine, other), jnp.where(first, other, mine)], axis=axis
    )


def after(values, *others):
    return lax.optimization_barrier((values, *others))[0]


def together(*values):
    return lax.optimization_barrier(values)


def gather_group(block):
    z, y, c = ctx_place()
    across = flip(block, CORES)
    near = flip(block, 1)
    far = flip(across, 1)
    found = jnp.zeros((LINES, CORES) + block.shape, block.dtype)
    for j, i, piece in ((0, 0, block), (0, 1, near), (1, 0, across), (1, 1, far)):
        found = lax.dynamic_update_slice(
            found, piece[None, None], (y ^ j, c ^ i) + (0,) * block.ndim
        )
    return found


def scatter_group(partial):
    z, y, c = ctx_place()
    near = flip(part(partial, 1 - c, 1), 1)
    chip = part(partial, c, 1).astype(jnp.float32) + near.astype(jnp.float32)
    across = flip(part(chip, 1 - y).astype(jnp.bfloat16), CORES)
    return part(chip, y) + across.astype(jnp.float32)


def gather_planes(piece):
    z, y, c = ctx_place()
    planes = plane_count()
    found = jnp.zeros((planes,) + piece.shape, piece.dtype)
    for k in [0] + plane_order():
        moved = shift(piece, k) if k else piece
        found = lax.dynamic_update_slice(
            found, moved[None], ((z - k) % planes,) + (0,) * piece.ndim
        )
    return found


def scatter_planes(partial):
    z, y, c = ctx_place()
    planes = plane_count()
    total = part(partial, z)
    for k in plane_order():
        away = part(partial, (z - k) % planes).astype(jnp.bfloat16)
        total = total + shift(away, -k).astype(jnp.float32)
    return total


def gather_ctx(block):
    z, y, c = ctx_place()
    planes = plane_count()
    found = jnp.zeros((planes, LINES, CORES) + block.shape, block.dtype)
    lines = {0: block}
    for k in plane_order():
        lines[k] = shift(block, k)
    for k in [0] + plane_order():
        chips = (lines[k], flip(lines[k], CORES))
        for j in range(LINES):
            for i, piece in enumerate((chips[j], flip(chips[j], 1))):
                place = ((z - k) % planes, y ^ j, c ^ i) + (0,) * block.ndim
                found = lax.dynamic_update_slice(found, piece[None, None, None], place)
    return found.reshape((-1,) + block.shape[1:])


def scatter_ctx(partial, works):
    z, y, c = ctx_place()
    planes = plane_count()
    rows = partial.shape[0] // (planes * CHIP)
    partial = partial.reshape(planes, LINES, CORES, rows, partial.shape[1])
    order = plane_order()[::-1] + [0]
    blocks = {k: part(partial, (z - k) % planes) for k in order}
    near = {k: flip(part(blocks[k], 1 - c, 1), 1) for k in order}
    chip, across = {}, {}
    for k in order:
        chip[k] = part(blocks[k], c, 1).astype(jnp.float32) + near[k].astype(jnp.float32)
    sent = {k: part(chip[k], 1 - y).astype(jnp.bfloat16) for k in order}
    for k in order:
        across[k] = flip(sent[k], CORES)
    results = [works[0]([sent[k] for k in order])]
    total, moved = None, ()
    for step, k in enumerate(order):
        line = after(part(chip[k], y), *moved, *results[-1]) + across[k].astype(jnp.float32)
        if k:
            away = line.astype(jnp.bfloat16)
            moved = (shift(away, -k),)
            line = moved[0].astype(jnp.float32)
            if step + 1 < len(works):
                results.append(works[step + 1]([away]))
        total = line if total is None else total + line
    return total, [value for result in results for value in result]


def gather_small(values):
    z, y, c = ctx_place()
    both = pair(values, flip(values, 1), c, 0)
    plane = pair(both, flip(both, CORES), y, 0)
    return gather_planes(plane).reshape((-1,) + values.shape)


def peer_block(block):
    return swap(block) if lax.axis_size("fsdp") == 2 else gather_fsdp(block, 1)


def gather_fsdp(block, axis):
    if lax.axis_size("fsdp") != 2:
        return lax.all_gather(block, "fsdp", axis=axis, tiled=True)
    peer = swap(block)
    first = lax.axis_index("fsdp") == 0
    return jnp.concatenate(
        [jnp.where(first, block, peer), jnp.where(first, peer, block)], axis=axis
    )


def send_fsdp(total, axis, *first):
    if lax.axis_size("fsdp") != 2:
        away = after(total.astype(jnp.bfloat16), *first)
        return None, lax.psum_scatter(away, "fsdp", scatter_dimension=axis, tiled=True), away
    here = lax.axis_index("fsdp")
    half = total.shape[axis] // 2
    away = lax.dynamic_slice_in_dim(total, (1 - here) * half, half, axis)
    kept = lax.dynamic_slice_in_dim(total, here * half, half, axis)
    away = after(away.astype(jnp.bfloat16), *first)
    return kept, swap(away), away


def add_fsdp(kept, arrived, away=None):
    arrived = arrived.astype(jnp.float32)
    return arrived if kept is None else kept.astype(jnp.float32) + arrived


def scatter_fsdp(total, axis):
    return add_fsdp(*send_fsdp(total, axis)[:2])


def deal_group(pack):
    z, y, c = ctx_place()
    lines = pair(part(pack, y, 1), flip(part(pack, 1 - y, 1), CORES), y, 0)
    return pair(part(lines, c, 2), flip(part(lines, 1 - c, 2), 1), c, 1)


def undeal_group(slices):
    z, y, c = ctx_place()
    cores = pair(part(slices, c, 1), flip(part(slices, 1 - c, 1), 1), c, 2)
    return pair(part(cores, y), flip(part(cores, 1 - y), CORES), y, 1)


def group_slice(pack):
    rows, count, size = pack.shape
    return deal_group(pack.reshape(rows, LINES, CORES, size)).reshape(CHIP, 1, rows, size)


def deal_planes(piece):
    z, y, c = ctx_place()
    planes = plane_count()
    size = piece.shape[-1] // planes
    found = jnp.zeros((planes,) + piece.shape[:-1] + (size,), piece.dtype)
    for k in [0] + plane_order():
        away = lax.dynamic_slice_in_dim(piece, (z + k) % planes * size, size, piece.ndim - 1)
        moved = shift(away, k) if k else away
        found = lax.dynamic_update_slice(
            found, moved[None], ((z - k) % planes,) + (0,) * piece.ndim
        )
    return found


def group_weights(piece, peer):
    z, y, c = ctx_place()
    planes, shards = plane_count(), lax.axis_size("fsdp")
    rows, size = piece.shape[2:]
    if shards != 2:
        return gather_planes(gather_fsdp(piece, 1)).reshape(-1, size)
    x = lax.axis_index("fsdp")
    found = jnp.zeros((planes, CHIP, shards, rows, size), piece.dtype)
    for k in [0] + plane_order():
        moved = shift(piece, k) if k else piece
        other = swap(moved) if k else peer
        for side, block in ((x, moved), (1 - x, other)):
            found = lax.dynamic_update_slice(
                found, block[None], ((z - k) % planes, 0, side, 0, 0)
            )
    return found.reshape(-1, size)


def send_grads(grad, *first):
    planes, shards = plane_count(), lax.axis_size("fsdp")
    rows = grad.shape[0] // (planes * CHIP * shards)
    return send_fsdp(grad.reshape(planes, CHIP, shards, rows, grad.shape[1]), 2, *first)


def plane_grads(kept, arrived):
    total = add_fsdp(kept, arrived)
    planes, place, shards, rows, size = total.shape
    return scatter_planes(total.reshape(planes, place, rows, size))


def sum_fsdp(total):
    return lax.psum_scatter(
        total.astype(jnp.bfloat16), "fsdp", scatter_dimension=0, tiled=True
    ).astype(jnp.float32)


def collected(kept, arrived, kind):
    moved = lax.all_to_all(
        add_fsdp(kept, arrived).astype(kind), "ctx", split_axis=0, concat_axis=0, tiled=True
    )
    return moved.astype(jnp.float32).transpose(1, 0, 2)


def dot32(spec, left, right):
    return jnp.einsum(spec, left, right, preferred_element_type=jnp.float32)


def chunks_of(size, step):
    return [(at, min(step, size - at)) for at in range(0, size, step)]


def dot_nt(left, right):
    return lax.dot_general(
        left, right, (((1,), (1,)), ((), ())), preferred_element_type=jnp.float32
    )


def dot_nn(left, right):
    return jnp.dot(left, right, preferred_element_type=jnp.float32)


def dot_tn(left, right):
    return lax.dot_general(
        left, right, (((0,), (0,)), ((), ())), preferred_element_type=jnp.float32
    )


def silu_parts(values):
    sigmoid_part = 0.5 + 0.5 * jnp.tanh(0.5 * values)
    return values * sigmoid_part, sigmoid_part * (1.0 + values * (1.0 - sigmoid_part))


def experts_kernel(
    tok, cot, named, place, place_t, mine, router, w_gate, w_up, w_down, s_gate, s_up, s_down,
    joint, received, slot_grad, hidden, grad_a, grad_b, shared_hidden, grad_sa,
    grad_sb, gates, slot_cot,
):
    low = jnp.bfloat16
    width, units = tok.shape[1], w_gate.shape[1]
    logits = dot_nn(tok[...], router[...])
    chosen = named[...] > 0
    peak = jnp.max(jnp.where(chosen, logits, -1e30), axis=1, keepdims=True)
    raised = jnp.where(chosen, jnp.exp(jnp.where(chosen, logits - peak, 0.0)), 0.0)
    shares = raised / jnp.sum(raised, axis=1, keepdims=True)
    gates[...] = shares
    own = jnp.dot(
        place[...].astype(jnp.float32),
        shares * mine[...],
        precision=highest,
        preferred_element_type=jnp.float32,
    )
    slot_gate = jnp.sum(own, axis=1, keepdims=True)

    step = 256
    for at, size in chunks_of(width, step):
        received[:, at : at + size] = dot_nn(place[...], tok[:, at : at + size]).astype(low)
        found = dot_nn(place[...], cot[:, at : at + size])
        slot_cot[:, at : at + size] = found.astype(low)
        slot_grad[:, at : at + size] = (slot_gate * found).astype(low)

    shared_a = dot_nn(tok[...], s_gate[...])
    shared_b = dot_nn(tok[...], s_up[...])
    act, slope = silu_parts(shared_a)
    shared_hidden[...] = (act * shared_b).astype(low)
    grad_sh = dot_nn(cot[...], s_down[...])
    grad_sa[...] = (grad_sh * shared_b * slope).astype(low)
    grad_sb[...] = (grad_sh * act).astype(low)

    def unit_step(at, size):
        value_a = dot_nn(received[...], w_gate[:, pl.ds(at, size)])
        value_b = dot_nn(received[...], w_up[:, pl.ds(at, size)])
        act, slope = silu_parts(value_a)
        hidden[:, pl.ds(at, size)] = (act * value_b).astype(low)
        grad_h = dot_nt(slot_grad[...], w_down[pl.ds(at, size), :])
        grad_a[:, pl.ds(at, size)] = (grad_h * value_b * slope).astype(low)
        grad_b[:, pl.ds(at, size)] = (grad_h * act).astype(low)

    whole = units // step

    def unit_loop(i, carry):
        unit_step(pl.multiple_of(i * step, step), step)
        return carry

    lax.fori_loop(0, whole, unit_loop, 0)
    if units % step:
        unit_step(whole * step, units % step)

    def width_loop(i, score):
        at = pl.multiple_of(i * step, step)
        here = pl.ds(at, step)
        row = dot_nt(grad_a[...], w_gate[here, :]) + dot_nt(grad_b[...], w_up[here, :])
        joint[:, here] = (
            dot_nn(place_t[...], row.astype(low))
            + dot_nt(grad_sa[...], s_gate[here, :])
            + dot_nt(grad_sb[...], s_up[here, :])
        ).astype(low)
        made = dot_nn(hidden[...], w_down[:, here]).astype(low).astype(jnp.float32)
        joint[:, pl.ds(width + at, step)] = (
            dot_nn(place_t[...], (slot_gate * made).astype(low))
            + dot_nt(shared_hidden[...], s_down[here, :])
        ).astype(low)
        return score + jnp.sum(slot_cot[:, here].astype(jnp.float32) * made, axis=1, keepdims=True)

    score = lax.fori_loop(
        0, width // step, width_loop, jnp.zeros((received.shape[0], 1), jnp.float32)
    )
    spread_score = jnp.dot(
        place_t[...].astype(jnp.float32),
        score * mine[...],
        precision=highest,
        preferred_element_type=jnp.float32,
    )
    joint[:, 2 * width :] = spread_score.astype(low)


def run_experts(rows_in, named, place, place_t, mine, router, weights, shared):
    count, slots, tile = place.shape
    width = rows_in.shape[1] // 2
    units, share = weights[0].shape[1], shared[0].shape[1]
    low = jnp.bfloat16

    def tiles(size, columns):
        return pl.BlockSpec((size, columns), lambda i: (i, 0))

    def whole(array):
        return pl.BlockSpec(
            array.shape, lambda i: (0,) * array.ndim, pipeline_mode=pl.Buffered(1)
        )

    outs = [
        (tile, 2 * width + 128, low),
        (slots, width, low),
        (slots, width, low),
        (slots, units, low),
        (slots, units, low),
        (slots, units, low),
        (tile, share, low),
        (tile, share, low),
        (tile, share, low),
        (tile, 128, jnp.float32),
    ]
    return pl.pallas_call(
        experts_kernel,
        grid=(count,),
        in_specs=[
            tiles(tile, width),
            pl.BlockSpec((tile, width), lambda i: (i, 1)),
            tiles(tile, 128),
            pl.BlockSpec((None, slots, tile), lambda i: (i, 0, 0)),
            pl.BlockSpec((None, tile, slots), lambda i: (i, 0, 0)),
            whole(mine),
            whole(router),
        ]
        + [whole(w) for w in weights + shared],
        out_specs=[tiles(size, columns) for size, columns, kind in outs],
        out_shape=[
            jax.ShapeDtypeStruct((count * size, columns), kind) for size, columns, kind in outs
        ],
        scratch_shapes=[pltpu.VMEM((slots, width), low)],
        compiler_params=pltpu.CompilerParams(vmem_limit_bytes=60 * 2**20),
        cost_estimate=pl.CostEstimate(flops=10**10, bytes_accessed=10**7, transcendentals=0),
    )(rows_in, rows_in, named, place, place_t, mine, router, *weights, *shared)


def outer_kernel(left, right, out):
    for at, size in chunks_of(right.shape[1], 256):
        out[:, at : at + size] = dot_tn(left[...], right[:, at : at + size]).astype(out.dtype)


def outer(left, right, first=0, height=None, kind=jnp.bfloat16):
    rows = left.shape[0]
    height = left.shape[1] if height is None else height
    columns = right.shape[1]
    tile = 256 if height % 256 == 0 else 128
    return pl.pallas_call(
        outer_kernel,
        grid=(height // tile,),
        in_specs=[
            pl.BlockSpec((rows, tile), lambda i: (0, i + first // tile)),
            pl.BlockSpec((rows, columns), lambda i: (0, 0), pipeline_mode=pl.Buffered(1)),
        ],
        out_specs=pl.BlockSpec((tile, columns), lambda i: (i, 0)),
        out_shape=jax.ShapeDtypeStruct((height, columns), kind),
        compiler_params=pltpu.CompilerParams(vmem_limit_bytes=40 * 2**20),
        cost_estimate=pl.CostEstimate(flops=10**6, bytes_accessed=10**4, transcendentals=0),
    )(left, right)


def attention_kernel(query, keys, values, own_pos, seq_pos, probs, attended):
    scale = HEAD_DIM ** (-0.5)
    rows = query.shape[0]
    step = 128
    for at in range(0, rows, step):
        here = slice(at, at + step)
        scores = dot_nt(query[here, :], keys[...]) * scale
        scores = jnp.where(own_pos[here, :] >= seq_pos[...], scores, -1e30)
        raised = jnp.exp(scores - jnp.max(scores, axis=1, keepdims=True))
        share = (raised * (1.0 / jnp.sum(raised, axis=1, keepdims=True))).astype(jnp.bfloat16)
        probs[here, :] = share
        attended[here, :] = dot_nn(share, values[...]).astype(jnp.bfloat16)


def run_attention(query, keys, values, own_pos, seq_pos):
    rows, wide = query.shape
    heads, length = wide // HEAD_DIM, keys.shape[0]

    def whole(array):
        return pl.BlockSpec(array.shape, lambda i: (0, 0))

    by_head = pl.BlockSpec((rows, HEAD_DIM), lambda i: (0, i))
    return pl.pallas_call(
        attention_kernel,
        grid=(heads,),
        in_specs=[by_head, whole(keys), whole(values), whole(own_pos), whole(seq_pos)],
        out_specs=[pl.BlockSpec((None, rows, length), lambda i: (i, 0, 0)), by_head],
        out_shape=[
            jax.ShapeDtypeStruct((heads, rows, length), jnp.bfloat16),
            jax.ShapeDtypeStruct((rows, wide), jnp.bfloat16),
        ],
        compiler_params=pltpu.CompilerParams(vmem_limit_bytes=40 * 2**20),
        cost_estimate=pl.CostEstimate(flops=10**6, bytes_accessed=10**4, transcendentals=0),
    )(query, keys, values, own_pos, seq_pos)


def attention_back_kernel(probs, grad, query, keys, values, grad_query, grad_both, grad_scores):
    scale = HEAD_DIM ** (-0.5)
    rows = query.shape[0]
    step = 128
    for at in range(0, rows, step):
        here = slice(at, at + step)
        grad_probs = dot_nt(grad[here, :], values[...])
        share = probs[here, :].astype(jnp.float32)
        row_dot = jnp.sum(share * grad_probs, axis=1, keepdims=True)
        low_scores = (share * (grad_probs - row_dot)).astype(jnp.bfloat16)
        grad_scores[here, :] = low_scores
        grad_query[here, :] = dot_nn(low_scores, keys[...]) * scale

    def add(part, value):
        @pl.when(pl.program_id(0) == 0)
        def _():
            grad_both[:, part] = value

        @pl.when(pl.program_id(0) != 0)
        def _():
            grad_both[:, part] += value

    add(slice(0, HEAD_DIM), dot_tn(grad_scores[...], query[...]) * scale)
    add(slice(HEAD_DIM, 2 * HEAD_DIM), dot_tn(probs[...], grad[...]))


def run_attention_back(probs, grad, query, keys, values):
    rows, wide = query.shape
    heads, length = wide // HEAD_DIM, keys.shape[0]

    def whole(array):
        return pl.BlockSpec(array.shape, lambda i: (0, 0))

    by_head = pl.BlockSpec((rows, HEAD_DIM), lambda i: (0, i))
    return pl.pallas_call(
        attention_back_kernel,
        grid=(heads,),
        in_specs=[
            pl.BlockSpec((None, rows, length), lambda i: (i, 0, 0)),
            by_head,
            by_head,
            whole(keys),
            whole(values),
        ],
        out_specs=[by_head, pl.BlockSpec((length, 2 * HEAD_DIM), lambda i: (0, 0))],
        out_shape=[
            jax.ShapeDtypeStruct((rows, wide), jnp.float32),
            jax.ShapeDtypeStruct((length, 2 * HEAD_DIM), jnp.float32),
        ],
        scratch_shapes=[pltpu.VMEM((rows, length), jnp.bfloat16)],
        compiler_params=pltpu.CompilerParams(vmem_limit_bytes=40 * 2**20),
        cost_estimate=pl.CostEstimate(flops=10**6, bytes_accessed=10**4, transcendentals=0),
    )(probs, grad, query, keys, values)


def body(
    inputs,
    gain_attn,
    w_query,
    w_key,
    w_value,
    w_out,
    gain_moe,
    w_router,
    shared_gate,
    shared_up,
    shared_down,
    expert_gate,
    expert_up,
    expert_down,
    positions,
    routes,
    cotangent,
):
    ctx_count = lax.axis_size("ctx")
    here = lax.axis_index("ctx")
    plane, line, core = ctx_place()
    tok_rows = inputs.shape[1]
    width = inputs.shape[2]
    group = HEADS // KV_HEADS
    scale = HEAD_DIM ** (-0.5)
    experts = w_router.shape[1]
    length = tok_rows * ctx_count
    part_rows = w_query.shape[0]
    capacity = min(tok_rows, 3 * tok_rows * TOP // (2 * experts))
    heads_wide = group * HEAD_DIM
    low = jnp.bfloat16

    narrow = jnp.concatenate([w_router, gain_attn[:, None], gain_moe[:, None]], axis=1)
    narrow = jnp.pad(narrow, ((0, 0), (0, HEAD_DIM - narrow.shape[1])))
    qkv_pack = jnp.concatenate(
        [
            w_query.reshape(part_rows, KV_HEADS, heads_wide),
            w_key.reshape(part_rows, KV_HEADS, HEAD_DIM),
            w_value.reshape(part_rows, KV_HEADS, HEAD_DIM),
            jnp.broadcast_to(narrow[:, None], (part_rows, KV_HEADS, HEAD_DIM)),
            w_out.T.reshape(part_rows, KV_HEADS, heads_wide),
        ],
        axis=2,
    )
    all_routes = gather_small(routes[0].T)
    piece = after(group_slice(qkv_pack), all_routes)
    group_in = gather_group(after(inputs[0], piece)).reshape(CHIP * tok_rows, width)
    peer = peer_block(piece)
    qkv_full = group_weights(piece, peer)
    hidden_part = shared_gate.shape[1] // ctx_count

    def unit_slices(weight):
        return weight.reshape(part_rows, plane_count(), CHIP, hidden_part)

    shared_pack = jnp.concatenate(
        [unit_slices(shared_gate), unit_slices(shared_up), unit_slices(shared_down.T)], axis=3
    )
    shared_piece = group_slice(
        after(shared_pack.transpose(0, 2, 1, 3).reshape(part_rows, CHIP, -1), piece)
    )
    seq_pos = positions[0]

    tile_rows = CHIP * tok_rows
    tile_slots = CHIP * capacity
    tile_count = length // tile_rows
    tile_routes = all_routes.transpose(0, 2, 1).reshape(tile_count, tile_rows, TOP)
    mine = jnp.any(tile_routes == here, axis=2).astype(jnp.int32)
    slot = jnp.where(mine > 0, jnp.cumsum(mine, axis=1) - 1, -1)
    slots = jnp.arange(tile_slots, dtype=jnp.int32)
    place = (slot[:, None, :] == slots[None, :, None]).astype(low)
    place_t = (slot[:, :, None] == slots[None, None, :]).astype(low)
    named = jnp.any(
        tile_routes.reshape(length, TOP, 1) == jnp.arange(128, dtype=jnp.int32), axis=1
    ).astype(jnp.float32)
    own_expert = (jnp.arange(128, dtype=jnp.int32) == here).astype(jnp.float32)[None]
    qkv_full = after(qkv_full, place, place_t, named, peer, shared_piece, group_in)
    qkv_wide = heads_wide + 2 * HEAD_DIM
    qkv_weight = qkv_full[:, :qkv_wide]
    router_wide = qkv_full[:, qkv_wide : qkv_wide + HEAD_DIM]
    out_weight = qkv_full[:, qkv_wide + HEAD_DIM :]
    router_weight = router_wide[:, :experts]
    gain_one = qkv_full[:, qkv_wide + experts].astype(jnp.float32)
    gain_two = qkv_full[:, qkv_wide + experts + 1].astype(jnp.float32)

    wide_in = group_in.astype(jnp.float32)
    inverse_one = lax.rsqrt(jnp.mean(wide_in * wide_in, axis=-1, keepdims=True) + epsilon)
    normed_in = wide_in * inverse_one
    attn_in = (normed_in * gain_one).astype(low)
    group_rows = CHIP * tok_rows
    group_pos = lax.dynamic_slice_in_dim(seq_pos, plane * group_rows, group_rows)
    cosine, sine_table = rope_tables(group_pos, HEAD_DIM)
    qkv = dot32("td,dh->th", attn_in, qkv_weight)
    keys_own = rotate(
        qkv[:, heads_wide : heads_wide + HEAD_DIM][:, None], cosine, sine_table
    )[:, 0].astype(low)
    values_own = qkv[:, heads_wide + HEAD_DIM :].astype(low)
    kv_own = jnp.concatenate([keys_own, values_own], axis=1)
    keys_values = gather_planes(kv_own).reshape(length, 2 * HEAD_DIM)
    routed_gate = lax.all_gather(after(expert_gate, qkv_full), "fsdp", axis=1, tiled=True)[0]
    routed_up = lax.all_gather(after(expert_up, qkv_full), "fsdp", axis=1, tiled=True)[0]
    routed_down = lax.all_gather(after(expert_down, qkv_full), "fsdp", axis=1, tiled=True)[0]
    keys, values = keys_values[:, :HEAD_DIM], keys_values[:, HEAD_DIM:]
    query = (
        rotate(qkv[:, :heads_wide].reshape(group_rows, group, HEAD_DIM), cosine, sine_table)
        .astype(low)
        .reshape(group_rows, heads_wide)
    )
    probs, attended = run_attention(
        query, keys, values, group_pos[:, None], seq_pos[None, :]
    )
    shared_rows = deal_planes(after(shared_piece, keys_values))
    state_part = dot32("th,dh->td", attended, out_weight).astype(low)
    token_in = inputs[0].astype(jnp.float32)
    state = token_in + scatter_group(state_part.reshape(LINES, CORES, tok_rows, width))

    inverse_two = lax.rsqrt(jnp.mean(state * state, axis=-1, keepdims=True) + epsilon)
    normed_two = state * inverse_two
    moe_in = (normed_two * gain_two).astype(low)
    if lax.axis_size("fsdp") == 2:
        shared_peer = swap(after(shared_rows, moe_in))
    all_rows = gather_ctx(jnp.concatenate([moe_in, cotangent[0]], axis=1))
    if lax.axis_size("fsdp") == 2:
        shared_peer = after(shared_peer, all_rows)
        first = lax.axis_index("fsdp") == 0
        shared_weight = jnp.concatenate(
            [
                jnp.where(first, shared_rows, shared_peer),
                jnp.where(first, shared_peer, shared_rows),
            ],
            axis=2,
        ).reshape(width, -1)
    else:
        shared_weight = gather_fsdp(shared_rows, 2).reshape(width, -1)
    shared_parts = [
        shared_weight[:, at * hidden_part : (at + 1) * hidden_part] for at in range(3)
    ]
    (
        joint_part,
        received,
        slot_grad,
        expert_hidden,
        grad_expert_a,
        grad_expert_b,
        shared_hidden,
        grad_shared_a,
        grad_shared_b,
        gates,
    ) = run_experts(
        all_rows,
        named,
        place,
        place_t,
        own_expert,
        router_wide,
        [routed_gate, routed_up, routed_down],
        shared_parts,
    )

    sent = {}

    sent["down"] = send_fsdp(outer(expert_hidden, slot_grad), 0)
    joint_part, down_away = together(joint_part, sent["down"][2])

    def first_work(values):
        held = after(received, *values)
        rows = after(all_rows, *values)
        gate = outer(held, grad_expert_a)
        sent["gate"] = send_fsdp(gate, 0, sent["down"][1])
        return gate, outer(rows, grad_shared_a, 0, width)

    def second_work(values):
        held = after(received, *values)
        rows = after(all_rows, *values)
        up = outer(held, grad_expert_b)
        sent["up"] = send_fsdp(up, 0, sent["gate"][1])
        return up, outer(rows, grad_shared_b, 0, width), sent["down"][1]

    def third_work(values):
        rows = after(all_rows, *values)
        return (outer(rows, shared_hidden, width, width),)

    joint_sum, weight_grads = scatter_ctx(joint_part, [first_work, second_work, third_work])
    grad_shared = jnp.concatenate(
        [weight_grads[1], weight_grads[3], weight_grads[5]], axis=1
    )
    sent["shared"] = send_fsdp(
        grad_shared.reshape(ctx_count, -1, 3 * hidden_part), 1, sent["up"][1]
    )
    grad_moe_sum = joint_sum[:, :width]
    output = (state + joint_sum[:, width : 2 * width]).astype(low)
    grad_gates = joint_sum[:, 2 * width : 2 * width + experts].T

    home_gates = part(gates.reshape(ctx_count, tok_rows, 128), here)[:, :experts].T
    gate_mean = jnp.sum(home_gates * grad_gates, axis=0, keepdims=True)
    grad_logits = home_gates * (grad_gates - gate_mean)
    grad_router = jnp.einsum(
        "td,et->de", moe_in.astype(jnp.float32), grad_logits, precision=highest
    )
    grad_moe_in = grad_moe_sum + jnp.einsum(
        "et,de->td", grad_logits, router_weight.astype(jnp.float32), precision=highest
    )
    grad_gain_two, grad_through = norm_back(grad_moe_in, normed_two, inverse_two, gain_two)
    grad_state = cotangent[0].astype(jnp.float32) + grad_through
    group_proj = gather_group(grad_state.astype(low)).reshape(group_rows, width)
    grad_expert_down = add_fsdp(*sent["down"])
    group_proj, output, grad_expert_down, gate_arrived = together(
        group_proj, output, grad_expert_down, sent["gate"][1]
    )

    grad_attended = dot32("td,dh->th", group_proj, out_weight).astype(low)
    out_sent = send_grads(dot32("td,th->dh", group_proj, attended), sent["shared"][1])
    grad_query_rot, grad_kv_part = run_attention_back(probs, grad_attended, query, keys, values)
    grad_query_rot = grad_query_rot.reshape(group_rows, group, HEAD_DIM)
    grad_expert_gate = add_fsdp(sent["gate"][0], gate_arrived)
    grad_kv_part, grad_expert_gate, up_arrived, out_arrived = together(
        grad_kv_part, grad_expert_gate, sent["up"][1], out_sent[1]
    )
    grad_keys_values = scatter_planes(
        grad_kv_part.reshape(plane_count(), group_rows, 2 * HEAD_DIM)
    )
    grad_expert_up = add_fsdp(sent["up"][0], up_arrived)
    out_planes = plane_grads(out_sent[0], out_arrived)
    grad_query_pre = (
        rotate(grad_query_rot, cosine, -sine_table).astype(low).reshape(group_rows, heads_wide)
    )
    query_sent = send_grads(dot32("td,th->dh", attn_in, grad_query_pre), out_arrived)
    grad_keys_values, grad_expert_up, query_arrived = together(
        grad_keys_values, grad_expert_up, query_sent[1]
    )
    query_planes = plane_grads(query_sent[0], query_arrived)
    grad_keys_pre = rotate(grad_keys_values[:, None, :HEAD_DIM], cosine, -sine_table)[:, 0]
    grad_kv_pre = jnp.concatenate(
        [grad_keys_pre.astype(low), grad_keys_values[:, HEAD_DIM:].astype(low)], axis=1
    )
    attn_part = dot32("th,dh->td", grad_query_pre, qkv_weight[:, :heads_wide]) + dot32(
        "th,dh->td", grad_kv_pre, qkv_weight[:, heads_wide:]
    )
    grad_attn_in = scatter_group(attn_part.astype(low).reshape(LINES, CORES, tok_rows, width))
    grad_gain_one = jnp.sum(attn_part * normed_in, axis=0)
    grad_kv = jnp.concatenate(
        [
            dot32("td,th->dh", attn_in, grad_kv_pre),
            grad_gain_one[:, None],
            grad_gain_two[:, None],
            jnp.pad(grad_router, ((0, 0), (0, HEAD_DIM - 2 - experts))),
        ],
        axis=1,
    )
    shared_back = collected(*sent["shared"][:2], low)
    back_gate = shared_back[:, :, :hidden_part].reshape(part_rows, -1)
    back_up = shared_back[:, :, hidden_part : 2 * hidden_part].reshape(part_rows, -1)
    back_down = shared_back[:, :, 2 * hidden_part :].reshape(part_rows, -1).T
    planes_sum = jnp.concatenate([query_planes, out_planes, plane_grads(*send_grads(grad_kv)[:2])], axis=2)
    planes_sum, grad_attn_in, back_gate, back_up, back_down = together(
        planes_sum, grad_attn_in, back_gate, back_up, back_down
    )
    all_back = undeal_group(
        planes_sum.astype(low).reshape(LINES, CORES, part_rows, planes_sum.shape[2])
    )
    all_back = all_back.reshape(part_rows, CHIP, -1).astype(jnp.float32)
    query_back = all_back[:, :, :heads_wide]
    out_back = all_back[:, :, heads_wide : 2 * heads_wide]
    kv_back = all_back[:, :, 2 * heads_wide :]
    narrow_back = jnp.sum(kv_back[:, :, 2 * HEAD_DIM :], axis=1)
    home_inverse = lax.rsqrt(jnp.mean(token_in * token_in, axis=-1, keepdims=True) + epsilon)
    unused, grad_first = norm_back(grad_attn_in, token_in * home_inverse, home_inverse, gain_one)
    grad_inputs = (grad_state + grad_first).astype(low)

    return (
        output[None],
        grad_inputs[None],
        narrow_back[:, 0],
        query_back.reshape(part_rows, -1),
        kv_back[:, :, :HEAD_DIM].reshape(part_rows, -1),
        kv_back[:, :, HEAD_DIM : 2 * HEAD_DIM].reshape(part_rows, -1),
        out_back.reshape(part_rows, -1).T,
        narrow_back[:, 1],
        narrow_back[:, 2 : 2 + experts],
        back_gate,
        back_up,
        back_down,
        grad_expert_gate[None],
        grad_expert_up[None],
        grad_expert_down[None],
    )


def solution(mesh):
    in_specs = (
        P("fsdp", "ctx", None),
        P(("ctx", "fsdp")),
        P(("ctx", "fsdp"), None),
        P(("ctx", "fsdp"), None),
        P(("ctx", "fsdp"), None),
        P(None, ("ctx", "fsdp")),
        P(("ctx", "fsdp")),
        P(("ctx", "fsdp"), None),
        P(("ctx", "fsdp"), None),
        P(("ctx", "fsdp"), None),
        P(None, ("ctx", "fsdp")),
        P("ctx", "fsdp", None),
        P("ctx", "fsdp", None),
        P("ctx", "fsdp", None),
        P("fsdp", None),
        P("fsdp", "ctx", None),
        P("fsdp", "ctx", None),
    )
    out_specs = (
        P("fsdp", "ctx", None),
        P("fsdp", "ctx", None),
        P(("ctx", "fsdp")),
        P(("ctx", "fsdp"), None),
        P(("ctx", "fsdp"), None),
        P(("ctx", "fsdp"), None),
        P(None, ("ctx", "fsdp")),
        P(("ctx", "fsdp")),
        P(("ctx", "fsdp"), None),
        P(("ctx", "fsdp"), None),
        P(("ctx", "fsdp"), None),
        P(None, ("ctx", "fsdp")),
        P("ctx", "fsdp", None),
        P("ctx", "fsdp", None),
        P("ctx", "fsdp", None),
    )
    return jax.shard_map(body, mesh=mesh, in_specs=in_specs, out_specs=out_specs, check_vma=False)
```

```python
import functools

import jax
import jax.numpy as jnp
from jax import lax
from jax.experimental import pallas as pl
from jax.experimental.pallas import tpu as pltpu
from jax.sharding import PartitionSpec as P

HEADS = 16
KV_HEADS = 4
HEAD_DIM = 128
TOP = 6


epsilon = 1e-06
rope_base = 600000.0
highest = lax.Precision.HIGHEST


def rope_tables(position_row, head_size):
    half_size = head_size // 2
    freq_steps = jnp.arange(half_size, dtype=jnp.float32)
    frequency = rope_base ** (-(freq_steps / half_size))
    angles = position_row.astype(jnp.float32)[:, None] * frequency[None, :]
    return (jnp.cos(angles), jnp.sin(angles))


def rotate(values, cosine, sine_table):
    half_size = values.shape[-1] // 2
    first_half = values[..., :half_size]
    second_half = values[..., half_size:]
    cosine_wide = cosine[:, None, :]
    sine_wide = sine_table[:, None, :]
    return jnp.concatenate(
        [
            first_half * cosine_wide - second_half * sine_wide,
            second_half * cosine_wide + first_half * sine_wide,
        ],
        axis=-1,
    )


def silu_slope(values):
    sigmoid_part = lax.logistic(values)
    return sigmoid_part * (1.0 + values * (1.0 - sigmoid_part))


def norm_back(grad_normed, normed, inverse, gain):
    grad_gain = jnp.sum(grad_normed * normed, axis=0)
    scaled = grad_normed * gain
    grad_values = inverse * (scaled - normed * jnp.mean(scaled * normed, axis=-1, keepdims=True))
    return (grad_gain, grad_values)


CORES = 2
LINES = 2
CHIP = CORES * LINES


def ctx_place():
    here = lax.axis_index("ctx")
    return here // CHIP, here // CORES % LINES, here % CORES


def plane_count():
    return lax.axis_size("ctx") // CHIP


def plane_order():
    planes = plane_count()
    return sorted(range(1, planes), key=lambda k: (min(k, planes - k), k))


def shift(values, step):
    planes = plane_count()
    pairs = [
        (i, (i // CHIP + step) % planes * CHIP + i % CHIP) for i in range(lax.axis_size("ctx"))
    ]
    return lax.ppermute(values, "ctx", pairs)


def flip(values, bit):
    return lax.ppermute(values, "ctx", [(i, i ^ bit) for i in range(lax.axis_size("ctx"))])


def swap(values):
    return lax.ppermute(values, "fsdp", [(0, 1), (1, 0)])


def part(values, index, axis=0):
    return lax.dynamic_index_in_dim(values, index, axis, keepdims=False)


def pair(mine, other, place, axis):
    first = place == 0
    return jnp.stack(
        [jnp.where(first, mine, other), jnp.where(first, other, mine)], axis=axis
    )


def after(values, *others):
    return lax.optimization_barrier((values, *others))[0]


def together(*values):
    return lax.optimization_barrier(values)


def gather_group(block):
    across = flip(block, CORES)
    return jnp.stack([block, across, flip(block, 1), flip(across, 1)])


def scatter_group(partial):
    near = flip(partial[1], 1)
    chip = partial[0].astype(jnp.float32) + near.astype(jnp.float32)
    across = flip(chip[1].astype(jnp.bfloat16), CORES)
    return chip[0] + across.astype(jnp.float32)


def flip_order(values, axis):
    z, y, c = ctx_place()
    lines = jnp.where(y == 0, values, jnp.flip(values, axis))
    cores = jnp.where(c == 0, lines, jnp.flip(lines, axis + 1))
    return jnp.swapaxes(cores, axis, axis + 1)


def gather_planes(piece):
    z, y, c = ctx_place()
    planes = plane_count()
    found = jnp.zeros((planes,) + piece.shape, piece.dtype)
    for k in [0] + plane_order():
        moved = shift(piece, k) if k else piece
        found = lax.dynamic_update_slice(
            found, moved[None], ((z - k) % planes,) + (0,) * piece.ndim
        )
    return found


def planes_away(partial):
    z, y, c = ctx_place()
    planes = plane_count()
    return {k: part(partial, (z - k) % planes).astype(jnp.bfloat16) for k in plane_order()}


def planes_total(own, arrived):
    for values in arrived:
        own = own + values.astype(jnp.float32)
    return own


def planes_sent(partial, away=None):
    away = planes_away(partial) if away is None else away
    return part(partial, ctx_place()[0]), [shift(away[k], -k) for k in plane_order()]


def scatter_planes(partial, away=None):
    return planes_total(*planes_sent(partial, away))


def plane_lines(block):
    return {k: shift(block, k) if k else block for k in [0] + plane_order()}


def gather_ctx(lines):
    planes = plane_count()
    found = {}
    for k in [0] + plane_order():
        chips = (lines[k], flip(lines[k], CORES))
        found[k] = chips + tuple(flip(piece, 1) for piece in chips)
    return jnp.concatenate([piece for k in range(planes) for piece in found[k]], axis=0)


def chip_step(keep, near, order, *first):
    planes = plane_count()
    near = flip(after(near, *first), 1)
    shape = (planes, LINES, keep.shape[0] // (planes * LINES), keep.shape[1])
    keep, near = keep.reshape(shape), near.reshape(shape)
    kept, sent, arrived = {}, {}, {}
    for k in order:
        kept[k] = keep[k, 0].astype(jnp.float32) + near[k, 0].astype(jnp.float32)
        chip = keep[k, 1].astype(jnp.float32) + near[k, 1].astype(jnp.float32)
        sent[k] = chip.astype(jnp.bfloat16)
        arrived[k] = flip(sent[k], CORES)
    return kept, sent, arrived


def scatter_two(partial, other, works, last):
    order = plane_order()[::-1] + [0]
    kept, sent, arrived = chip_step(*partial, order)
    other_kept, other_sent, other_arrived = chip_step(*other, order, *[sent[k] for k in order])
    results = [works[0]([sent[k] for k in order] + [other_sent[k] for k in order])]
    total, moved = None, ()
    for step, k in enumerate(order):
        ready = [other_arrived[order[step - 2]]] if step > 1 else []
        if not k:
            ready = ready + last()
        line = after(kept[k], *moved, *results[-1], *ready) + arrived[k].astype(jnp.float32)
        if k:
            away = line.astype(jnp.bfloat16)
            moved = (shift(away, -k),)
            line = moved[0].astype(jnp.float32)
            if step + 1 < len(works):
                results.append(works[step + 1]([away]))
        total = line if total is None else total + line

    def other_rows(reached):
        total = None
        for k in order:
            line = after(other_kept[k], reached) + other_arrived[k].astype(jnp.float32)
            if k:
                moved = shift(line.astype(jnp.bfloat16), -k)
                reached = yield moved
                line = moved.astype(jnp.float32)
            total = line if total is None else total + line
        yield total

    return total, [value for result in results for value in result], other_rows


def gather_small(values):
    both = jnp.stack([values, flip(values, 1)])
    plane = jnp.stack([both, flip(both, CORES)], axis=1)
    found = {0: plane}
    for k in plane_order():
        found[k] = shift(plane, k)
    return jnp.stack([found[k] for k in range(plane_count())]).reshape((-1,) + values.shape)


def peer_block(block):
    return swap(block) if lax.axis_size("fsdp") == 2 else gather_fsdp(block, 1)


def gather_fsdp(block, axis):
    if lax.axis_size("fsdp") != 2:
        return lax.all_gather(block, "fsdp", axis=axis, tiled=True)
    peer = swap(block)
    first = lax.axis_index("fsdp") == 0
    return jnp.concatenate(
        [jnp.where(first, block, peer), jnp.where(first, peer, block)], axis=axis
    )


def send_fsdp(total, axis, *first):
    if lax.axis_size("fsdp") != 2:
        away = after(total.astype(jnp.bfloat16), *first)
        return None, lax.psum_scatter(away, "fsdp", scatter_dimension=axis, tiled=True), away
    here = lax.axis_index("fsdp")
    half = total.shape[axis] // 2
    away = lax.dynamic_slice_in_dim(total, (1 - here) * half, half, axis)
    kept = lax.dynamic_slice_in_dim(total, here * half, half, axis)
    away = away.astype(jnp.bfloat16)
    return kept, swap(after(away, *first)), away


def add_fsdp(kept, arrived, away=None):
    arrived = arrived.astype(jnp.float32)
    return arrived if kept is None else kept.astype(jnp.float32) + arrived


def scatter_fsdp(total, axis):
    return add_fsdp(*send_fsdp(total, axis)[:2])


def deal_group(pack):
    z, y, c = ctx_place()
    lines = pair(part(pack, y, 1), flip(part(pack, 1 - y, 1), CORES), y, 0)
    return pair(part(lines, c, 2), flip(part(lines, 1 - c, 2), 1), c, 1)


def undeal_group(slices):
    z, y, c = ctx_place()
    cores = pair(part(slices, c, 1), flip(part(slices, 1 - c, 1), 1), c, 2)
    return pair(part(cores, y), flip(part(cores, 1 - y), CORES), y, 1)


def group_slice(pack):
    rows, count, size = pack.shape
    return deal_group(pack.reshape(rows, LINES, CORES, size)).reshape(CHIP, 1, rows, size)


def deal_planes(piece):
    z, y, c = ctx_place()
    planes = plane_count()
    size = piece.shape[-1] // planes
    found = jnp.zeros((planes,) + piece.shape[:-1] + (size,), piece.dtype)
    for k in [0] + plane_order():
        away = lax.dynamic_slice_in_dim(piece, (z + k) % planes * size, size, piece.ndim - 1)
        moved = shift(away, k) if k else away
        found = lax.dynamic_update_slice(
            found, moved[None], ((z - k) % planes,) + (0,) * piece.ndim
        )
    return found


def group_weights(piece, peer, *first):
    z, y, c = ctx_place()
    planes, shards = plane_count(), lax.axis_size("fsdp")
    rows, size = piece.shape[2:]
    if shards != 2:
        return gather_planes(gather_fsdp(piece, 1)).reshape(-1, size)
    x = lax.axis_index("fsdp")
    found = jnp.zeros((planes, CHIP, shards, rows, size), piece.dtype)
    for k in [0] + plane_order():
        moved = shift(piece, k) if k else piece
        other = swap(after(moved, other)) if k else after(peer, *first)
        for side, block in ((x, moved), (1 - x, other)):
            found = lax.dynamic_update_slice(
                found, block[None], ((z - k) % planes, 0, side, 0, 0)
            )
    return found.reshape(-1, size)


def send_grads(grad, *first):
    planes, shards = plane_count(), lax.axis_size("fsdp")
    rows = grad.shape[0] // (planes * CHIP * shards)
    return send_fsdp(grad.reshape(planes, CHIP, shards, rows, grad.shape[1]), 2, *first)


def grads_view(grad):
    planes, shards = plane_count(), lax.axis_size("fsdp")
    rows = grad.shape[0] // (planes * CHIP * shards)
    return grad.reshape(planes, CHIP, shards, rows, grad.shape[1])


def plane_view(total):
    planes, place, shards, rows, size = total.shape
    return total.reshape(planes, place, rows, size)


def sum_fsdp(total):
    return lax.psum_scatter(
        total.astype(jnp.bfloat16), "fsdp", scatter_dimension=0, tiled=True
    ).astype(jnp.float32)


def collected(kept, arrived, kind):
    moved = lax.all_to_all(
        add_fsdp(kept, arrived).astype(kind), "ctx", split_axis=0, concat_axis=0, tiled=True
    )
    return moved.astype(jnp.float32).transpose(1, 0, 2)


def dot32(spec, left, right):
    return jnp.einsum(spec, left, right, preferred_element_type=jnp.float32)


def chunks_of(size, step):
    return [(at, min(step, size - at)) for at in range(0, size, step)]


def dot_nt(left, right):
    return lax.dot_general(
        left, right, (((1,), (1,)), ((), ())), preferred_element_type=jnp.float32
    )


def dot_nn(left, right):
    return jnp.dot(left, right, preferred_element_type=jnp.float32)


def dot_tn(left, right):
    return lax.dot_general(
        left, right, (((0,), (0,)), ((), ())), preferred_element_type=jnp.float32
    )


def silu_parts(values):
    sigmoid_part = 0.5 + 0.5 * jnp.tanh(0.5 * values)
    return values * sigmoid_part, sigmoid_part * (1.0 + values * (1.0 - sigmoid_part))


def experts_kernel(
    piece,
    tok, cot, named, place, place_t, mine, router, w_gate, w_gate_late, w_up, w_down, s_gate, s_up, s_down,
    moe_keep, moe_near, out_keep, out_near, received, slot_grad, hidden, grad_a, grad_b, shared_hidden, grad_sa,
    grad_sb, gates, slot_cot,
):
    low = jnp.bfloat16
    width, units = tok.shape[1], w_gate.shape[1]
    half = tok.shape[0] // 2
    gates_in = (w_gate, w_gate_late)
    logits = dot_nn(tok[...], router[...])
    chosen = named[...] > 0
    peak = jnp.max(jnp.where(chosen, logits, -1e30), axis=1, keepdims=True)
    raised = jnp.where(chosen, jnp.exp(jnp.where(chosen, logits - peak, 0.0)), 0.0)
    shares = raised / jnp.sum(raised, axis=1, keepdims=True)
    gates[...] = shares
    own = jnp.dot(
        place[...].astype(jnp.float32),
        shares * mine[...],
        precision=highest,
        preferred_element_type=jnp.float32,
    )
    slot_gate = jnp.sum(own, axis=1, keepdims=True)

    step = 256
    for at, size in chunks_of(width, step):
        received[:, at : at + size] = dot_nn(place[...], tok[:, at : at + size]).astype(low)
        found = dot_nn(place[...], cot[:, at : at + size])
        slot_cot[:, at : at + size] = found.astype(low)
        slot_grad[:, at : at + size] = (slot_gate * found).astype(low)

    shared_a = dot_nn(tok[...], s_gate[...])
    shared_b = dot_nn(tok[...], s_up[...])
    act, slope = silu_parts(shared_a)
    shared_hidden[...] = (act * shared_b).astype(low)
    grad_sh = dot_nn(cot[...], s_down[...])
    grad_sa[...] = (grad_sh * shared_b * slope).astype(low)
    grad_sb[...] = (grad_sh * act).astype(low)

    def unit_step(at, size):
        value_a = 0.0
        for j in range(width // piece):
            rows = slice(j // 2 * piece, (j // 2 + 1) * piece)
            value_a = value_a + dot_nn(
                received[:, j * piece : (j + 1) * piece], gates_in[j % 2][rows, pl.ds(at, size)]
            )
        value_b = dot_nn(received[...], w_up[:, pl.ds(at, size)])
        act, slope = silu_parts(value_a)
        hidden[:, pl.ds(at, size)] = (act * value_b).astype(low)
        grad_h = dot_nt(slot_grad[...], w_down[pl.ds(at, size), :])
        grad_a[:, pl.ds(at, size)] = (grad_h * value_b * slope).astype(low)
        grad_b[:, pl.ds(at, size)] = (grad_h * act).astype(low)

    for at, size in chunks_of(units, 1408):
        unit_step(at, size)

    step = piece

    def width_loop(i, score):
        at = i * step
        here = pl.ds(at, step)
        gate_rows = gates_in[i % 2][i // 2 * step : (i // 2 + 1) * step, :]
        row = dot_nt(grad_a[...], gate_rows) + dot_nt(grad_b[...], w_up[here, :])
        part = (
            dot_nn(place_t[...], row.astype(low))
            + dot_nt(grad_sa[...], s_gate[here, :])
            + dot_nt(grad_sb[...], s_up[here, :])
        ).astype(low)
        moe_keep[:, here] = part[:half]
        moe_near[:, here] = part[half:]
        made = dot_nn(hidden[...], w_down[:, here]).astype(low).astype(jnp.float32)
        part = (
            dot_nn(place_t[...], (slot_gate * made).astype(low))
            + dot_nt(shared_hidden[...], s_down[here, :])
        ).astype(low)
        out_keep[:, here] = part[:half]
        out_near[:, here] = part[half:]
        return score + jnp.sum(slot_cot[:, here].astype(jnp.float32) * made, axis=1, keepdims=True)

    score = jnp.zeros((received.shape[0], 1), jnp.float32)
    for i in range(width // step):
        score = width_loop(i, score)
    spread_score = jnp.dot(
        place_t[...].astype(jnp.float32),
        score * mine[...],
        precision=highest,
        preferred_element_type=jnp.float32,
    )
    moe_keep[:, width:] = spread_score[:half].astype(low)
    moe_near[:, width:] = spread_score[half:].astype(low)


def run_experts(tok, cot, named, place, place_t, mine, router, weights, shared):
    count, slots, tile = place.shape
    width = tok.shape[1]
    units, share = weights[0].shape[1], shared[0].shape[1]
    low = jnp.bfloat16

    def tiles(size, columns):
        return pl.BlockSpec((size, columns), lambda i: (i, 0))

    def whole(array):
        return pl.BlockSpec(
            array.shape, lambda i: (0,) * array.ndim, pipeline_mode=pl.Buffered(1)
        )

    outs = [
        (tile // 2, width + 128, low),
        (tile // 2, width + 128, low),
        (tile // 2, width, low),
        (tile // 2, width, low),
        (slots, width, low),
        (slots, width, low),
        (slots, units, low),
        (slots, units, low),
        (slots, units, low),
        (tile, share, low),
        (tile, share, low),
        (tile, share, low),
        (tile, 128, jnp.float32),
    ]
    piece = weights[0].shape[0] // lax.axis_size("fsdp")
    return pl.pallas_call(
        functools.partial(experts_kernel, piece),
        grid=(count,),
        in_specs=[
            tiles(tile, width),
            tiles(tile, width),
            tiles(tile, 128),
            pl.BlockSpec((None, slots, tile), lambda i: (i, 0, 0)),
            pl.BlockSpec((None, tile, slots), lambda i: (i, 0, 0)),
            whole(mine),
            whole(router),
        ]
        + [whole(w) for w in weights + shared],
        out_specs=[tiles(size, columns) for size, columns, kind in outs],
        out_shape=[
            jax.ShapeDtypeStruct((count * size, columns), kind) for size, columns, kind in outs
        ],
        scratch_shapes=[pltpu.VMEM((slots, width), low)],
        compiler_params=pltpu.CompilerParams(vmem_limit_bytes=60 * 2**20),
        cost_estimate=pl.CostEstimate(flops=10**10, bytes_accessed=10**7, transcendentals=0),
    )(tok, cot, named, place, place_t, mine, router, *weights, *shared)


def outer_kernel(left, right, out):
    for at, size in chunks_of(right.shape[1], 256):
        out[:, at : at + size] = dot_tn(left[...], right[:, at : at + size]).astype(out.dtype)


def outer(left, right, kind=jnp.bfloat16):
    rows, height = left.shape
    columns = right.shape[1]
    tile = 256 if height % 256 == 0 else 128
    return pl.pallas_call(
        outer_kernel,
        grid=(height // tile,),
        in_specs=[
            pl.BlockSpec((rows, tile), lambda i: (0, i)),
            pl.BlockSpec((rows, columns), lambda i: (0, 0), pipeline_mode=pl.Buffered(1)),
        ],
        out_specs=pl.BlockSpec((tile, columns), lambda i: (i, 0)),
        out_shape=jax.ShapeDtypeStruct((height, columns), kind),
        compiler_params=pltpu.CompilerParams(vmem_limit_bytes=40 * 2**20),
        cost_estimate=pl.CostEstimate(flops=10**6, bytes_accessed=10**4, transcendentals=0),
    )(left, right)


def attention_kernel(query, keys, values, own_pos, seq_pos, probs, attended):
    scale = HEAD_DIM ** (-0.5)
    rows = query.shape[0]
    step = 128
    for at in range(0, rows, step):
        here = slice(at, at + step)
        scores = dot_nt(query[here, :], keys[...]) * scale
        scores = jnp.where(own_pos[here, :] >= seq_pos[...], scores, -1e30)
        raised = jnp.exp(scores - jnp.max(scores, axis=1, keepdims=True))
        share = (raised * (1.0 / jnp.sum(raised, axis=1, keepdims=True))).astype(jnp.bfloat16)
        probs[here, :] = share
        attended[here, :] = dot_nn(share, values[...]).astype(jnp.bfloat16)


def run_attention(query, keys, values, own_pos, seq_pos):
    rows, wide = query.shape
    heads, length = wide // HEAD_DIM, keys.shape[0]

    def whole(array):
        return pl.BlockSpec(array.shape, lambda i: (0, 0))

    by_head = pl.BlockSpec((rows, HEAD_DIM), lambda i: (0, i))
    return pl.pallas_call(
        attention_kernel,
        grid=(heads,),
        in_specs=[by_head, whole(keys), whole(values), whole(own_pos), whole(seq_pos)],
        out_specs=[pl.BlockSpec((None, rows, length), lambda i: (i, 0, 0)), by_head],
        out_shape=[
            jax.ShapeDtypeStruct((heads, rows, length), jnp.bfloat16),
            jax.ShapeDtypeStruct((rows, wide), jnp.bfloat16),
        ],
        compiler_params=pltpu.CompilerParams(vmem_limit_bytes=40 * 2**20),
        cost_estimate=pl.CostEstimate(flops=10**6, bytes_accessed=10**4, transcendentals=0),
    )(query, keys, values, own_pos, seq_pos)


def attention_back_kernel(probs, grad, query, keys, values, grad_query, grad_both, grad_scores):
    scale = HEAD_DIM ** (-0.5)
    rows = query.shape[0]
    step = 128
    for at in range(0, rows, step):
        here = slice(at, at + step)
        grad_probs = dot_nt(grad[here, :], values[...])
        share = probs[here, :].astype(jnp.float32)
        row_dot = jnp.sum(share * grad_probs, axis=1, keepdims=True)
        low_scores = (share * (grad_probs - row_dot)).astype(jnp.bfloat16)
        grad_scores[here, :] = low_scores
        grad_query[here, :] = dot_nn(low_scores, keys[...]) * scale

    def add(part, value):
        @pl.when(pl.program_id(0) == 0)
        def _():
            grad_both[:, part] = value

        @pl.when(pl.program_id(0) != 0)
        def _():
            grad_both[:, part] += value

    add(slice(0, HEAD_DIM), dot_tn(grad_scores[...], query[...]) * scale)
    add(slice(HEAD_DIM, 2 * HEAD_DIM), dot_tn(probs[...], grad[...]))


def run_attention_back(probs, grad, query, keys, values):
    rows, wide = query.shape
    heads, length = wide // HEAD_DIM, keys.shape[0]

    def whole(array):
        return pl.BlockSpec(array.shape, lambda i: (0, 0))

    by_head = pl.BlockSpec((rows, HEAD_DIM), lambda i: (0, i))
    return pl.pallas_call(
        attention_back_kernel,
        grid=(heads,),
        in_specs=[
            pl.BlockSpec((None, rows, length), lambda i: (i, 0, 0)),
            by_head,
            by_head,
            whole(keys),
            whole(values),
        ],
        out_specs=[by_head, pl.BlockSpec((length, 2 * HEAD_DIM), lambda i: (0, 0))],
        out_shape=[
            jax.ShapeDtypeStruct((rows, wide), jnp.float32),
            jax.ShapeDtypeStruct((length, 2 * HEAD_DIM), jnp.float32),
        ],
        scratch_shapes=[pltpu.VMEM((rows, length), jnp.bfloat16)],
        compiler_params=pltpu.CompilerParams(vmem_limit_bytes=40 * 2**20),
        cost_estimate=pl.CostEstimate(flops=10**6, bytes_accessed=10**4, transcendentals=0),
    )(probs, grad, query, keys, values)


def body(
    inputs,
    gain_attn,
    w_query,
    w_key,
    w_value,
    w_out,
    gain_moe,
    w_router,
    shared_gate,
    shared_up,
    shared_down,
    expert_gate,
    expert_up,
    expert_down,
    positions,
    routes,
    cotangent,
):
    ctx_count = lax.axis_size("ctx")
    here = lax.axis_index("ctx")
    plane, line, core = ctx_place()
    tok_rows = inputs.shape[1]
    width = inputs.shape[2]
    group = HEADS // KV_HEADS
    scale = HEAD_DIM ** (-0.5)
    experts = w_router.shape[1]
    length = tok_rows * ctx_count
    part_rows = w_query.shape[0]
    capacity = min(tok_rows, 3 * tok_rows * TOP // (2 * experts))
    heads_wide = group * HEAD_DIM
    low = jnp.bfloat16

    narrow = jnp.concatenate([w_router, gain_attn[:, None], gain_moe[:, None]], axis=1)
    narrow = jnp.pad(narrow, ((0, 0), (0, HEAD_DIM - narrow.shape[1])))
    qkv_pack = jnp.concatenate(
        [
            w_query.reshape(part_rows, KV_HEADS, heads_wide),
            w_key.reshape(part_rows, KV_HEADS, HEAD_DIM),
            w_value.reshape(part_rows, KV_HEADS, HEAD_DIM),
            jnp.broadcast_to(narrow[:, None], (part_rows, KV_HEADS, HEAD_DIM)),
            w_out.T.reshape(part_rows, KV_HEADS, heads_wide),
        ],
        axis=2,
    )
    all_routes = gather_small(routes[0].T)
    piece = after(group_slice(qkv_pack), all_routes)
    group_in = gather_group(after(inputs[0], piece)).reshape(CHIP * tok_rows, width)
    peer = peer_block(piece)
    qkv_full = group_weights(piece, peer, group_in)
    hidden_part = shared_gate.shape[1] // ctx_count

    def unit_slices(weight):
        return weight.reshape(part_rows, plane_count(), CHIP, hidden_part)

    shared_pack = jnp.concatenate(
        [unit_slices(shared_gate), unit_slices(shared_up), unit_slices(shared_down.T)], axis=3
    )
    shared_piece = group_slice(
        after(shared_pack.transpose(0, 2, 1, 3).reshape(part_rows, CHIP, -1), piece)
    )
    seq_pos = flip_order(
        positions[0].reshape(plane_count(), LINES, CORES, tok_rows), 1
    ).reshape(length)

    tile_rows = CHIP * tok_rows
    tile_slots = CHIP * capacity
    tile_count = length // tile_rows
    tile_routes = all_routes.transpose(0, 2, 1).reshape(tile_count, tile_rows, TOP)
    mine = jnp.any(tile_routes == here, axis=2).astype(jnp.int32)
    slot = jnp.where(mine > 0, jnp.cumsum(mine, axis=1) - 1, -1)
    slots = jnp.arange(tile_slots, dtype=jnp.int32)
    place = (slot[:, None, :] == slots[None, :, None]).astype(low)
    place_t = (slot[:, :, None] == slots[None, None, :]).astype(low)
    named = jnp.any(
        tile_routes.reshape(length, TOP, 1) == jnp.arange(128, dtype=jnp.int32), axis=1
    ).astype(jnp.float32)
    own_expert = (jnp.arange(128, dtype=jnp.int32) == here).astype(jnp.float32)[None]
    qkv_full = after(qkv_full, place, place_t, named, peer, shared_piece, group_in)
    qkv_wide = heads_wide + 2 * HEAD_DIM
    qkv_weight = qkv_full[:, :qkv_wide]
    router_wide = qkv_full[:, qkv_wide : qkv_wide + HEAD_DIM]
    out_weight = qkv_full[:, qkv_wide + HEAD_DIM :]
    router_weight = router_wide[:, :experts]
    gain_one = qkv_full[:, qkv_wide + experts].astype(jnp.float32)
    gain_two = qkv_full[:, qkv_wide + experts + 1].astype(jnp.float32)

    wide_in = group_in.astype(jnp.float32)
    inverse_one = lax.rsqrt(jnp.mean(wide_in * wide_in, axis=-1, keepdims=True) + epsilon)
    normed_in = wide_in * inverse_one
    attn_in = (normed_in * gain_one).astype(low)
    group_rows = CHIP * tok_rows
    group_pos = lax.dynamic_slice_in_dim(seq_pos, plane * group_rows, group_rows)
    cosine, sine_table = rope_tables(group_pos, HEAD_DIM)
    qkv = dot32("td,dh->th", attn_in, qkv_weight)
    keys_own = rotate(
        qkv[:, heads_wide : heads_wide + HEAD_DIM][:, None], cosine, sine_table
    )[:, 0].astype(low)
    values_own = qkv[:, heads_wide + HEAD_DIM :].astype(low)
    kv_own = jnp.concatenate([keys_own, values_own], axis=1)
    keys_values = gather_planes(kv_own).reshape(length, 2 * HEAD_DIM)
    gate_half = expert_gate.shape[1] // 2
    gate_first = lax.all_gather(expert_gate[:, :gate_half], "fsdp", axis=1, tiled=True)[0]
    gate_second = lax.all_gather(
        after(expert_gate[:, gate_half:], qkv_full), "fsdp", axis=1, tiled=True
    )[0]
    routed_up = lax.all_gather(after(expert_up, qkv_full), "fsdp", axis=1, tiled=True)[0]
    routed_down = lax.all_gather(after(expert_down, qkv_full), "fsdp", axis=1, tiled=True)[0]
    keys, values = keys_values[:, :HEAD_DIM], keys_values[:, HEAD_DIM:]
    query = (
        rotate(qkv[:, :heads_wide].reshape(group_rows, group, HEAD_DIM), cosine, sine_table)
        .astype(low)
        .reshape(group_rows, heads_wide)
    )
    probs, attended = run_attention(
        query, keys, values, group_pos[:, None], seq_pos[None, :]
    )
    shared_rows = deal_planes(after(shared_piece, kv_own))
    attended = after(attended, shared_rows)
    state_part = dot32("th,dh->td", attended, out_weight).astype(low)
    token_in = inputs[0].astype(jnp.float32)
    state = token_in + scatter_group(state_part.reshape(CORES, LINES, tok_rows, width))

    inverse_two = lax.rsqrt(jnp.mean(state * state, axis=-1, keepdims=True) + epsilon)
    normed_two = state * inverse_two
    moe_in = (normed_two * gain_two).astype(low)
    if lax.axis_size("fsdp") == 2:
        shared_peer = swap(after(shared_rows, attended))
    moe_lines = plane_lines(moe_in)
    all_moe = gather_ctx(moe_lines)
    cot_lines = plane_lines(after(cotangent[0], keys_values))
    all_cot = gather_ctx({k: after(line, moe_in) for k, line in cot_lines.items()})
    if lax.axis_size("fsdp") == 2:
        shared_peer = after(shared_peer, moe_lines[plane_order()[-1]])
        first = lax.axis_index("fsdp") == 0
        shared_weight = jnp.concatenate(
            [
                jnp.where(first, shared_rows, shared_peer),
                jnp.where(first, shared_peer, shared_rows),
            ],
            axis=2,
        ).reshape(width, -1)
    else:
        shared_weight = gather_fsdp(shared_rows, 2).reshape(width, -1)
    shared_parts = [
        shared_weight[:, at * hidden_part : (at + 1) * hidden_part] for at in range(3)
    ]
    (
        moe_keep,
        moe_near,
        out_keep,
        out_near,
        received,
        slot_grad,
        expert_hidden,
        grad_expert_a,
        grad_expert_b,
        shared_hidden,
        grad_shared_a,
        grad_shared_b,
        gates,
    ) = run_experts(
        all_moe,
        all_cot,
        named,
        place,
        place_t,
        own_expert,
        router_wide,
        [gate_first, gate_second, routed_up, routed_down],
        shared_parts,
    )

    sent = {}

    sent["down"] = send_fsdp(outer(expert_hidden, slot_grad), 0)

    def first_work(values):
        held = after(received, *values)
        rows = after(all_moe, *values)
        return outer(held, grad_expert_a), outer(rows, grad_shared_a)

    def second_work(values):
        up = outer(after(received, *values), grad_expert_b)
        sent["gate"] = send_fsdp(works_done[0], 0, sent["down"][1], up)
        sent["up"] = send_fsdp(up, 0, sent["gate"][1])
        return up, sent["gate"][2]

    def third_work(values):
        rows = after(all_moe, *values)
        grad_shared = jnp.concatenate(
            [
                after(works_done[1], *values),
                outer(rows, grad_shared_b),
                outer(after(all_cot, *values), shared_hidden),
            ],
            axis=1,
        )
        sent["shared"] = send_fsdp(
            grad_shared.reshape(ctx_count, -1, 3 * hidden_part), 1, sent["up"][1]
        )
        return (grad_shared,)

    works_done = {}

    def keep_first(values):
        done = first_work(values)
        works_done[0], works_done[1] = done
        return done

    moe_sum, weight_grads, out_rows = scatter_two(
        (moe_keep, moe_near),
        (out_keep, out_near),
        [keep_first, second_work, third_work],
        lambda: [sent["gate"][1]],
    )
    out_steps = out_rows(moe_sum)
    out_moved = [next(out_steps)]
    for unused in plane_order()[1:]:
        out_moved.append(out_steps.send(moe_sum))
    grad_moe_sum = moe_sum[:, :width]
    grad_gates = moe_sum[:, width : width + experts].T

    home_gates = gates[:tok_rows, :experts].T
    gate_mean = jnp.sum(home_gates * grad_gates, axis=0, keepdims=True)
    grad_logits = home_gates * (grad_gates - gate_mean)
    grad_router = jnp.einsum(
        "td,et->de", moe_in.astype(jnp.float32), grad_logits, precision=highest
    )
    grad_moe_in = grad_moe_sum + jnp.einsum(
        "et,de->td", grad_logits, router_weight.astype(jnp.float32), precision=highest
    )
    grad_gain_two, grad_through = norm_back(grad_moe_in, normed_two, inverse_two, gain_two)
    grad_state = cotangent[0].astype(jnp.float32) + grad_through
    group_proj = gather_group(grad_state.astype(low)).reshape(group_rows, width)
    grad_expert_down = add_fsdp(*sent["down"])
    group_proj, grad_expert_down = together(group_proj, grad_expert_down)

    grad_attended = dot32("td,dh->th", group_proj, out_weight).astype(low)
    grad_query_rot, grad_kv_part = run_attention_back(probs, grad_attended, query, keys, values)
    grad_query_rot = grad_query_rot.reshape(group_rows, group, HEAD_DIM)
    grad_expert_gate = add_fsdp(*sent["gate"])
    grad_kv_part, *unused = together(grad_kv_part, *out_moved, sent["up"][1])
    up_arrived = sent["up"][1]
    grad_kv_part = grad_kv_part.reshape(plane_count(), group_rows, 2 * HEAD_DIM)
    kv_away = planes_away(grad_kv_part)
    grad_keys_values = scatter_planes(grad_kv_part, away=kv_away)
    grad_expert_up = add_fsdp(sent["up"][0], up_arrived)
    grad_query_pre = (
        rotate(grad_query_rot, cosine, -sine_table).astype(low).reshape(group_rows, heads_wide)
    )
    query_sent = send_grads(
        dot32("td,th->dh", attn_in, grad_query_pre), sent["shared"][1]
    )
    grad_keys_values, grad_expert_gate, *unused = together(
        grad_keys_values, grad_expert_gate, sent["shared"][1]
    )
    grad_keys_pre = rotate(grad_keys_values[:, None, :HEAD_DIM], cosine, -sine_table)[:, 0]
    grad_kv_pre = jnp.concatenate(
        [grad_keys_pre.astype(low), grad_keys_values[:, HEAD_DIM:].astype(low)], axis=1
    )
    attn_part = dot32("th,dh->td", grad_query_pre, qkv_weight[:, :heads_wide]) + dot32(
        "th,dh->td", grad_kv_pre, qkv_weight[:, heads_wide:]
    )
    grad_attn_in = scatter_group(attn_part.astype(low).reshape(CORES, LINES, tok_rows, width))
    grad_gain_one = jnp.sum(attn_part * normed_in, axis=0)
    grad_kv = jnp.concatenate(
        [
            dot32("td,th->dh", attn_in, grad_kv_pre),
            grad_gain_one[:, None],
            grad_gain_two[:, None],
            jnp.pad(grad_router, ((0, 0), (0, HEAD_DIM - 2 - experts))),
        ],
        axis=1,
    )
    shared_back = collected(*sent["shared"][:2], low)
    grad_kv = after(grad_kv, grad_attn_in)
    kv_sent = send_grads(grad_kv, query_sent[1])
    query_planes = scatter_planes(
        plane_view(add_fsdp(query_sent[0], after(query_sent[1], kv_sent[2])))
    )
    back_gate = shared_back[:, :, :hidden_part].reshape(part_rows, -1)
    back_up = shared_back[:, :, hidden_part : 2 * hidden_part].reshape(part_rows, -1)
    back_down = shared_back[:, :, 2 * hidden_part :].reshape(part_rows, -1).T
    output = (state + out_steps.send(grad_keys_values)).astype(low)
    kv_arrived = after(kv_sent[1], back_gate, back_up, back_down, output, grad_expert_up)
    kv_total = plane_view(add_fsdp(kv_sent[0], kv_arrived))
    out_own, out_arrived = planes_sent(
        grads_view(dot32("td,th->dh", group_proj, after(attended, *kv_away.values())))
    )
    kv_total, out_own = together(kv_total, out_own)
    kv_planes = scatter_planes(kv_total)
    out_planes = planes_total(out_own, out_arrived)
    planes_sum = jnp.concatenate(
        [query_planes, scatter_fsdp(out_planes, 1)[:, 0], kv_planes], axis=2
    )
    planes_sum, grad_attn_in, back_gate, back_up, back_down, output = together(
        planes_sum, grad_attn_in, back_gate, back_up, back_down, output
    )
    all_back = undeal_group(
        planes_sum.astype(low).reshape(LINES, CORES, part_rows, planes_sum.shape[2])
    )
    all_back = all_back.reshape(part_rows, CHIP, -1).astype(jnp.float32)
    query_back = all_back[:, :, :heads_wide]
    out_back = all_back[:, :, heads_wide : 2 * heads_wide]
    kv_back = all_back[:, :, 2 * heads_wide :]
    narrow_back = jnp.sum(kv_back[:, :, 2 * HEAD_DIM :], axis=1)
    home_inverse = lax.rsqrt(jnp.mean(token_in * token_in, axis=-1, keepdims=True) + epsilon)
    unused, grad_first = norm_back(grad_attn_in, token_in * home_inverse, home_inverse, gain_one)
    grad_inputs = (grad_state + grad_first).astype(low)

    return (
        output[None],
        grad_inputs[None],
        narrow_back[:, 0],
        query_back.reshape(part_rows, -1),
        kv_back[:, :, :HEAD_DIM].reshape(part_rows, -1),
        kv_back[:, :, HEAD_DIM : 2 * HEAD_DIM].reshape(part_rows, -1),
        out_back.reshape(part_rows, -1).T,
        narrow_back[:, 1],
        narrow_back[:, 2 : 2 + experts],
        back_gate,
        back_up,
        back_down,
        grad_expert_gate[None],
        grad_expert_up[None],
        grad_expert_down[None],
    )


def solution(mesh):
    in_specs = (
        P("fsdp", "ctx", None),
        P(("ctx", "fsdp")),
        P(("ctx", "fsdp"), None),
        P(("ctx", "fsdp"), None),
        P(("ctx", "fsdp"), None),
        P(None, ("ctx", "fsdp")),
        P(("ctx", "fsdp")),
        P(("ctx", "fsdp"), None),
        P(("ctx", "fsdp"), None),
        P(("ctx", "fsdp"), None),
        P(None, ("ctx", "fsdp")),
        P("ctx", "fsdp", None),
        P("ctx", "fsdp", None),
        P("ctx", "fsdp", None),
        P("fsdp", None),
        P("fsdp", "ctx", None),
        P("fsdp", "ctx", None),
    )
    out_specs = (
        P("fsdp", "ctx", None),
        P("fsdp", "ctx", None),
        P(("ctx", "fsdp")),
        P(("ctx", "fsdp"), None),
        P(("ctx", "fsdp"), None),
        P(("ctx", "fsdp"), None),
        P(None, ("ctx", "fsdp")),
        P(("ctx", "fsdp")),
        P(("ctx", "fsdp"), None),
        P(("ctx", "fsdp"), None),
        P(("ctx", "fsdp"), None),
        P(None, ("ctx", "fsdp")),
        P("ctx", "fsdp", None),
        P("ctx", "fsdp", None),
        P("ctx", "fsdp", None),
    )
    return jax.shard_map(body, mesh=mesh, in_specs=in_specs, out_specs=out_specs, check_vma=False)
```

```python
import functools

import jax
import jax.numpy as jnp
from jax import lax
from jax.experimental import pallas as pl
from jax.experimental.pallas import tpu as pltpu
from jax.sharding import PartitionSpec as P

HEADS = 16
KV_HEADS = 4
HEAD_DIM = 128
TOP = 6


epsilon = 1e-06
rope_base = 600000.0
highest = lax.Precision.HIGHEST


def rope_tables(position_row, head_size):
    half_size = head_size // 2
    freq_steps = jnp.arange(half_size, dtype=jnp.float32)
    frequency = rope_base ** (-(freq_steps / half_size))
    angles = position_row.astype(jnp.float32)[:, None] * frequency[None, :]
    return (jnp.cos(angles), jnp.sin(angles))


def rotate(values, cosine, sine_table):
    half_size = values.shape[-1] // 2
    first_half = values[..., :half_size]
    second_half = values[..., half_size:]
    cosine_wide = cosine[:, None, :]
    sine_wide = sine_table[:, None, :]
    return jnp.concatenate(
        [
            first_half * cosine_wide - second_half * sine_wide,
            second_half * cosine_wide + first_half * sine_wide,
        ],
        axis=-1,
    )


def silu_slope(values):
    sigmoid_part = lax.logistic(values)
    return sigmoid_part * (1.0 + values * (1.0 - sigmoid_part))


def norm_back(grad_normed, normed, inverse, gain):
    grad_gain = jnp.sum(grad_normed * normed, axis=0)
    scaled = grad_normed * gain
    grad_values = inverse * (scaled - normed * jnp.mean(scaled * normed, axis=-1, keepdims=True))
    return (grad_gain, grad_values)


CORES = 2
LINES = 2
CHIP = CORES * LINES


def ctx_place():
    here = lax.axis_index("ctx")
    return here // CHIP, here // CORES % LINES, here % CORES


def plane_count():
    return lax.axis_size("ctx") // CHIP


def plane_order():
    planes = plane_count()
    return sorted(range(1, planes), key=lambda k: (min(k, planes - k), k))


def shift(values, step):
    planes = plane_count()
    pairs = [
        (i, (i // CHIP + step) % planes * CHIP + i % CHIP) for i in range(lax.axis_size("ctx"))
    ]
    return lax.ppermute(values, "ctx", pairs)


def flip(values, bit):
    return lax.ppermute(values, "ctx", [(i, i ^ bit) for i in range(lax.axis_size("ctx"))])


def swap(values):
    return lax.ppermute(values, "fsdp", [(0, 1), (1, 0)])


def part(values, index, axis=0):
    return lax.dynamic_index_in_dim(values, index, axis, keepdims=False)


def pair(mine, other, place, axis):
    first = place == 0
    return jnp.stack(
        [jnp.where(first, mine, other), jnp.where(first, other, mine)], axis=axis
    )


def after(values, *others):
    return lax.optimization_barrier((values, *others))[0]


def together(*values):
    return lax.optimization_barrier(values)


def gather_group(block):
    across = flip(block, CORES)
    return jnp.stack([block, across, flip(block, 1), flip(across, 1)])


def scatter_group(partial):
    near = flip(partial[1], 1)
    chip = partial[0].astype(jnp.float32) + near.astype(jnp.float32)
    across = flip(chip[1].astype(jnp.bfloat16), CORES)
    return chip[0] + across.astype(jnp.float32)


def flip_order(values, axis):
    z, y, c = ctx_place()
    lines = jnp.where(y == 0, values, jnp.flip(values, axis))
    cores = jnp.where(c == 0, lines, jnp.flip(lines, axis + 1))
    return jnp.swapaxes(cores, axis, axis + 1)


def gather_planes(piece):
    z, y, c = ctx_place()
    planes = plane_count()
    found = jnp.zeros((planes,) + piece.shape, piece.dtype)
    for k in [0] + plane_order():
        moved = shift(piece, k) if k else piece
        found = lax.dynamic_update_slice(
            found, moved[None], ((z - k) % planes,) + (0,) * piece.ndim
        )
    return found


def planes_away(partial):
    z, y, c = ctx_place()
    planes = plane_count()
    return {k: part(partial, (z - k) % planes).astype(jnp.bfloat16) for k in plane_order()}


def planes_total(own, arrived):
    for values in arrived:
        own = own + values.astype(jnp.float32)
    return own


def planes_sent(partial, away=None):
    away = planes_away(partial) if away is None else away
    return part(partial, ctx_place()[0]), [shift(away[k], -k) for k in plane_order()]


def scatter_planes(partial, away=None):
    return planes_total(*planes_sent(partial, away))


def plane_lines(block):
    return {k: shift(block, k) if k else block for k in [0] + plane_order()}


def gather_ctx(lines):
    planes = plane_count()
    found = {}
    for k in [0] + plane_order():
        chips = (lines[k], flip(lines[k], CORES))
        found[k] = chips + tuple(flip(piece, 1) for piece in chips)
    return jnp.concatenate([piece for k in range(planes) for piece in found[k]], axis=0)


def chip_step(keep, near, order, *first):
    planes = plane_count()
    near = flip(after(near, *first), 1)
    shape = (planes, LINES, keep.shape[0] // (planes * LINES), keep.shape[1])
    keep, near = keep.reshape(shape), near.reshape(shape)
    kept, sent, arrived = {}, {}, {}
    for k in order:
        kept[k] = keep[k, 0].astype(jnp.float32) + near[k, 0].astype(jnp.float32)
        chip = keep[k, 1].astype(jnp.float32) + near[k, 1].astype(jnp.float32)
        sent[k] = chip.astype(jnp.bfloat16)
        arrived[k] = flip(sent[k], CORES)
    return kept, sent, arrived


def scatter_two(partial, other, works, last):
    order = plane_order()[::-1] + [0]
    kept, sent, arrived = chip_step(*partial, order)
    other_kept, other_sent, other_arrived = chip_step(*other, order, *[sent[k] for k in order])
    results = [works[0]([sent[k] for k in order] + [other_sent[k] for k in order])]
    total, moved = None, ()
    for step, k in enumerate(order):
        ready = [other_arrived[order[step - 2]]] if step > 1 else []
        if not k:
            ready = ready + last()
        line = after(kept[k], *moved, *results[-1], *ready) + arrived[k].astype(jnp.float32)
        if k:
            away = line.astype(jnp.bfloat16)
            moved = (shift(away, -k),)
            line = moved[0].astype(jnp.float32)
            if step + 1 < len(works):
                results.append(works[step + 1]([away]))
        total = line if total is None else total + line

    def other_rows(reached):
        total = None
        for k in order:
            line = after(other_kept[k], reached) + other_arrived[k].astype(jnp.float32)
            if k:
                moved = shift(line.astype(jnp.bfloat16), -k)
                reached = yield moved
                line = moved.astype(jnp.float32)
            total = line if total is None else total + line
        yield total

    return total, [value for result in results for value in result], other_rows


def gather_small(values):
    both = jnp.stack([values, flip(values, 1)])
    plane = jnp.stack([both, flip(both, CORES)], axis=1)
    found = {0: plane}
    for k in plane_order():
        found[k] = shift(plane, k)
    return jnp.stack([found[k] for k in range(plane_count())]).reshape((-1,) + values.shape)


def peer_block(block):
    return swap(block) if lax.axis_size("fsdp") == 2 else gather_fsdp(block, 1)


def gather_fsdp(block, axis):
    if lax.axis_size("fsdp") != 2:
        return lax.all_gather(block, "fsdp", axis=axis, tiled=True)
    peer = swap(block)
    first = lax.axis_index("fsdp") == 0
    return jnp.concatenate(
        [jnp.where(first, block, peer), jnp.where(first, peer, block)], axis=axis
    )


def send_fsdp(total, axis, *first):
    if lax.axis_size("fsdp") != 2:
        away = after(total.astype(jnp.bfloat16), *first)
        return None, lax.psum_scatter(away, "fsdp", scatter_dimension=axis, tiled=True), away
    here = lax.axis_index("fsdp")
    half = total.shape[axis] // 2
    away = lax.dynamic_slice_in_dim(total, (1 - here) * half, half, axis)
    kept = lax.dynamic_slice_in_dim(total, here * half, half, axis)
    away = away.astype(jnp.bfloat16)
    return kept, swap(after(away, *first)), away


def add_fsdp(kept, arrived, away=None):
    arrived = arrived.astype(jnp.float32)
    return arrived if kept is None else kept.astype(jnp.float32) + arrived


def scatter_fsdp(total, axis):
    return add_fsdp(*send_fsdp(total, axis)[:2])


def deal_group(pack):
    z, y, c = ctx_place()
    lines = pair(part(pack, y, 1), flip(part(pack, 1 - y, 1), CORES), y, 0)
    return pair(part(lines, c, 2), flip(part(lines, 1 - c, 2), 1), c, 1)


def undeal_group(slices):
    z, y, c = ctx_place()
    cores = pair(part(slices, c, 1), flip(part(slices, 1 - c, 1), 1), c, 2)
    return pair(part(cores, y), flip(part(cores, 1 - y), CORES), y, 1)


def group_slice(pack):
    rows, count, size = pack.shape
    return deal_group(pack.reshape(rows, LINES, CORES, size)).reshape(CHIP, 1, rows, size)


def deal_planes(piece):
    z, y, c = ctx_place()
    planes = plane_count()
    size = piece.shape[-1] // planes
    found = jnp.zeros((planes,) + piece.shape[:-1] + (size,), piece.dtype)
    for k in [0] + plane_order():
        away = lax.dynamic_slice_in_dim(piece, (z + k) % planes * size, size, piece.ndim - 1)
        moved = shift(away, k) if k else away
        found = lax.dynamic_update_slice(
            found, moved[None], ((z - k) % planes,) + (0,) * piece.ndim
        )
    return found


def group_weights(piece, peer, *first):
    z, y, c = ctx_place()
    planes, shards = plane_count(), lax.axis_size("fsdp")
    rows, size = piece.shape[2:]
    if shards != 2:
        return gather_planes(gather_fsdp(piece, 1)).reshape(-1, size)
    x = lax.axis_index("fsdp")
    found = jnp.zeros((planes, CHIP, shards, rows, size), piece.dtype)
    for k in [0] + plane_order():
        moved = shift(piece, k) if k else piece
        other = swap(after(moved, other)) if k else after(peer, *first)
        for side, block in ((x, moved), (1 - x, other)):
            found = lax.dynamic_update_slice(
                found, block[None], ((z - k) % planes, 0, side, 0, 0)
            )
    return found.reshape(-1, size)


def send_grads(grad, *first):
    planes, shards = plane_count(), lax.axis_size("fsdp")
    rows = grad.shape[0] // (planes * CHIP * shards)
    return send_fsdp(grad.reshape(planes, CHIP, shards, rows, grad.shape[1]), 2, *first)


def grads_view(grad):
    planes, shards = plane_count(), lax.axis_size("fsdp")
    rows = grad.shape[0] // (planes * CHIP * shards)
    return grad.reshape(planes, CHIP, shards, rows, grad.shape[1])


def plane_view(total):
    planes, place, shards, rows, size = total.shape
    return total.reshape(planes, place, rows, size)


def sum_fsdp(total):
    return lax.psum_scatter(
        total.astype(jnp.bfloat16), "fsdp", scatter_dimension=0, tiled=True
    ).astype(jnp.float32)


def collected(kept, arrived, kind):
    moved = lax.all_to_all(
        add_fsdp(kept, arrived).astype(kind), "ctx", split_axis=0, concat_axis=0, tiled=True
    )
    return moved.astype(jnp.float32).transpose(1, 0, 2)


def dot32(spec, left, right):
    return jnp.einsum(spec, left, right, preferred_element_type=jnp.float32)


def chunks_of(size, step):
    return [(at, min(step, size - at)) for at in range(0, size, step)]


def dot_nt(left, right):
    return lax.dot_general(
        left, right, (((1,), (1,)), ((), ())), preferred_element_type=jnp.float32
    )


def dot_nn(left, right):
    return jnp.dot(left, right, preferred_element_type=jnp.float32)


def dot_tn(left, right):
    return lax.dot_general(
        left, right, (((0,), (0,)), ((), ())), preferred_element_type=jnp.float32
    )


def silu_parts(values):
    sigmoid_part = 0.5 + 0.5 * jnp.tanh(0.5 * values)
    return values * sigmoid_part, sigmoid_part * (1.0 + values * (1.0 - sigmoid_part))


def experts_kernel(
    piece,
    tok, cot, named, place, place_t, mine, router, far_gate, far_late, far_up, far_down, s_gate, s_up, s_down,
    moe_keep, moe_near, out_keep, out_near, received, slot_grad, hidden, grad_a, grad_b, shared_hidden, grad_sa,
    grad_sb, gates, slot_cot,
    w_gate, w_gate_late, w_up, w_down, arrived,
):
    low = jnp.bfloat16
    width, units = tok.shape[1], w_gate.shape[1]
    copies = [
        pltpu.make_async_copy(far, near, arrived.at[j])
        for j, (far, near) in enumerate(
            ((far_gate, w_gate), (far_late, w_gate_late), (far_up, w_up), (far_down, w_down))
        )
    ]

    @pl.when(pl.program_id(0) == 0)
    def _():
        for copy in copies:
            copy.start()

    half, rows = tok.shape[0] // 2, place.shape[1]
    low_rows, high_rows = slice(0, rows), slice(rows, 2 * rows)
    halves = ((slice(0, half), low_rows), (slice(half, 2 * half), high_rows))
    gates_in = (w_gate, w_gate_late)
    logits = dot_nn(tok[...], router[...])
    chosen = named[...] > 0
    peak = jnp.max(jnp.where(chosen, logits, -1e30), axis=1, keepdims=True)
    raised = jnp.where(chosen, jnp.exp(jnp.where(chosen, logits - peak, 0.0)), 0.0)
    shares = raised / jnp.sum(raised, axis=1, keepdims=True)
    gates[...] = shares
    own = [
        jnp.dot(
            place[h].astype(jnp.float32),
            (shares * mine[...])[toks],
            precision=highest,
            preferred_element_type=jnp.float32,
        )
        for h, (toks, picks) in enumerate(halves)
    ]
    slot_gate = jnp.sum(jnp.concatenate(own, axis=0), axis=1, keepdims=True)

    step = 256
    for at, size in chunks_of(width, step):
        for h, (toks, picks) in enumerate(halves):
            received[picks, at : at + size] = dot_nn(place[h], tok[toks, at : at + size]).astype(low)
            found = dot_nn(place[h], cot[toks, at : at + size])
            slot_cot[picks, at : at + size] = found.astype(low)
            slot_grad[picks, at : at + size] = (slot_gate[picks] * found).astype(low)

    shared_a = dot_nn(tok[...], s_gate[...])
    shared_b = dot_nn(tok[...], s_up[...])
    act, slope = silu_parts(shared_a)
    shared_hidden[...] = (act * shared_b).astype(low)
    grad_sh = dot_nn(cot[...], s_down[...])
    grad_sa[...] = (grad_sh * shared_b * slope).astype(low)
    grad_sb[...] = (grad_sh * act).astype(low)

    @pl.when(pl.program_id(0) == 0)
    def _():
        for copy in copies:
            copy.wait()

    def unit_step(at, size):
        value_a = 0.0
        for j in range(width // piece):
            rows = slice(j // 2 * piece, (j // 2 + 1) * piece)
            value_a = value_a + dot_nn(
                received[:, j * piece : (j + 1) * piece], gates_in[j % 2][rows, pl.ds(at, size)]
            )
        value_b = dot_nn(received[...], w_up[:, pl.ds(at, size)])
        act, slope = silu_parts(value_a)
        hidden[:, pl.ds(at, size)] = (act * value_b).astype(low)
        grad_h = dot_nt(slot_grad[...], w_down[pl.ds(at, size), :])
        grad_a[:, pl.ds(at, size)] = (grad_h * value_b * slope).astype(low)
        grad_b[:, pl.ds(at, size)] = (grad_h * act).astype(low)

    for at, size in chunks_of(units, 1408):
        unit_step(at, size)

    step = piece

    def width_loop(i, score):
        at = i * step
        here = pl.ds(at, step)
        gate_rows = gates_in[i % 2][i // 2 * step : (i // 2 + 1) * step, :]
        row = dot_nt(grad_a[...], gate_rows) + dot_nt(grad_b[...], w_up[here, :])
        row = row.astype(low)
        for h, (toks, picks) in enumerate(halves):
            (moe_keep, moe_near)[h][:, here] = (
                dot_nn(place_t[h], row[picks])
                + dot_nt(grad_sa[toks, :], s_gate[here, :])
                + dot_nt(grad_sb[toks, :], s_up[here, :])
            ).astype(low)
        made = dot_nn(hidden[...], w_down[:, here]).astype(low).astype(jnp.float32)
        row = (slot_gate * made).astype(low)
        for h, (toks, picks) in enumerate(halves):
            (out_keep, out_near)[h][:, here] = (
                dot_nn(place_t[h], row[picks]) + dot_nt(shared_hidden[toks, :], s_down[here, :])
            ).astype(low)
        return score + jnp.sum(slot_cot[:, here].astype(jnp.float32) * made, axis=1, keepdims=True)

    score = jnp.zeros((received.shape[0], 1), jnp.float32)
    for i in range(width // step):
        score = width_loop(i, score)
    for h, (toks, picks) in enumerate(halves):
        (moe_keep, moe_near)[h][:, width:] = jnp.dot(
            place_t[h].astype(jnp.float32),
            score[picks] * mine[...],
            precision=highest,
            preferred_element_type=jnp.float32,
        ).astype(low)


def run_experts(tok, cot, named, place, place_t, mine, router, weights, shared):
    count, slots, tile = place.shape[0] // 2, 2 * place.shape[1], 2 * place.shape[2]
    width = tok.shape[1]
    units, share = weights[0].shape[1], shared[0].shape[1]
    low = jnp.bfloat16

    def tiles(size, columns):
        return pl.BlockSpec((size, columns), lambda i: (i, 0))

    def whole(array):
        return pl.BlockSpec(
            array.shape, lambda i: (0,) * array.ndim, pipeline_mode=pl.Buffered(1)
        )

    outs = [
        (tile // 2, width + 128, low),
        (tile // 2, width + 128, low),
        (tile // 2, width, low),
        (tile // 2, width, low),
        (slots, width, low),
        (slots, width, low),
        (slots, units, low),
        (slots, units, low),
        (slots, units, low),
        (tile, share, low),
        (tile, share, low),
        (tile, share, low),
        (tile, 128, jnp.float32),
    ]
    piece = weights[0].shape[0] // lax.axis_size("fsdp")
    return pl.pallas_call(
        functools.partial(experts_kernel, piece),
        grid=(count,),
        in_specs=[
            tiles(tile, width),
            tiles(tile, width),
            tiles(tile, 128),
            pl.BlockSpec((2,) + place.shape[1:], lambda i: (i, 0, 0)),
            pl.BlockSpec((2,) + place_t.shape[1:], lambda i: (i, 0, 0)),
            whole(mine),
            whole(router),
        ]
        + [pl.BlockSpec(memory_space=pl.ANY) for w in weights]
        + [whole(w) for w in shared],
        out_specs=[tiles(size, columns) for size, columns, kind in outs],
        out_shape=[
            jax.ShapeDtypeStruct((count * size, columns), kind) for size, columns, kind in outs
        ],
        scratch_shapes=[pltpu.VMEM((slots, width), low)]
        + [pltpu.VMEM(w.shape, low) for w in weights]
        + [pltpu.SemaphoreType.DMA((len(weights),))],
        compiler_params=pltpu.CompilerParams(vmem_limit_bytes=60 * 2**20),
        cost_estimate=pl.CostEstimate(flops=10**10, bytes_accessed=10**7, transcendentals=0),
    )(tok, cot, named, place, place_t, mine, router, *weights, *shared)


def outer_kernel(left, right, out):
    for at, size in chunks_of(right.shape[1], 256):
        out[:, at : at + size] = dot_tn(left[...], right[:, at : at + size]).astype(out.dtype)


def outer(left, right, kind=jnp.bfloat16):
    rows, height = left.shape
    columns = right.shape[1]
    tile = 256 if height % 256 == 0 else 128
    return pl.pallas_call(
        outer_kernel,
        grid=(height // tile,),
        in_specs=[
            pl.BlockSpec((rows, tile), lambda i: (0, i)),
            pl.BlockSpec((rows, columns), lambda i: (0, 0), pipeline_mode=pl.Buffered(1)),
        ],
        out_specs=pl.BlockSpec((tile, columns), lambda i: (i, 0)),
        out_shape=jax.ShapeDtypeStruct((height, columns), kind),
        compiler_params=pltpu.CompilerParams(vmem_limit_bytes=40 * 2**20),
        cost_estimate=pl.CostEstimate(flops=10**6, bytes_accessed=10**4, transcendentals=0),
    )(left, right)


def attention_kernel(query, keys, values, own_pos, seq_pos, probs, attended):
    scale = HEAD_DIM ** (-0.5)
    rows = query.shape[0]
    step = 128
    for at in range(0, rows, step):
        here = slice(at, at + step)
        scores = dot_nt(query[here, :], keys[...]) * scale
        scores = jnp.where(own_pos[here, :] >= seq_pos[...], scores, -1e30)
        raised = jnp.exp(scores - jnp.max(scores, axis=1, keepdims=True))
        share = (raised * (1.0 / jnp.sum(raised, axis=1, keepdims=True))).astype(jnp.bfloat16)
        probs[here, :] = share
        attended[here, :] = dot_nn(share, values[...]).astype(jnp.bfloat16)


def run_attention(query, keys, values, own_pos, seq_pos):
    rows, wide = query.shape
    heads, length = wide // HEAD_DIM, keys.shape[0]

    def whole(array):
        return pl.BlockSpec(array.shape, lambda i: (0, 0))

    by_head = pl.BlockSpec((rows, HEAD_DIM), lambda i: (0, i))
    return pl.pallas_call(
        attention_kernel,
        grid=(heads,),
        in_specs=[by_head, whole(keys), whole(values), whole(own_pos), whole(seq_pos)],
        out_specs=[pl.BlockSpec((None, rows, length), lambda i: (i, 0, 0)), by_head],
        out_shape=[
            jax.ShapeDtypeStruct((heads, rows, length), jnp.bfloat16),
            jax.ShapeDtypeStruct((rows, wide), jnp.bfloat16),
        ],
        compiler_params=pltpu.CompilerParams(vmem_limit_bytes=40 * 2**20),
        cost_estimate=pl.CostEstimate(flops=10**6, bytes_accessed=10**4, transcendentals=0),
    )(query, keys, values, own_pos, seq_pos)


def attention_back_kernel(probs, grad, query, keys, values, grad_query, grad_both, grad_scores):
    scale = HEAD_DIM ** (-0.5)
    rows = query.shape[0]
    step = 128
    for at in range(0, rows, step):
        here = slice(at, at + step)
        grad_probs = dot_nt(grad[here, :], values[...])
        share = probs[here, :].astype(jnp.float32)
        row_dot = jnp.sum(share * grad_probs, axis=1, keepdims=True)
        low_scores = (share * (grad_probs - row_dot)).astype(jnp.bfloat16)
        grad_scores[here, :] = low_scores
        grad_query[here, :] = dot_nn(low_scores, keys[...]) * scale

    def add(part, value):
        @pl.when(pl.program_id(0) == 0)
        def _():
            grad_both[:, part] = value

        @pl.when(pl.program_id(0) != 0)
        def _():
            grad_both[:, part] += value

    add(slice(0, HEAD_DIM), dot_tn(grad_scores[...], query[...]) * scale)
    add(slice(HEAD_DIM, 2 * HEAD_DIM), dot_tn(probs[...], grad[...]))


def run_attention_back(probs, grad, query, keys, values):
    rows, wide = query.shape
    heads, length = wide // HEAD_DIM, keys.shape[0]

    def whole(array):
        return pl.BlockSpec(array.shape, lambda i: (0, 0))

    by_head = pl.BlockSpec((rows, HEAD_DIM), lambda i: (0, i))
    return pl.pallas_call(
        attention_back_kernel,
        grid=(heads,),
        in_specs=[
            pl.BlockSpec((None, rows, length), lambda i: (i, 0, 0)),
            by_head,
            by_head,
            whole(keys),
            whole(values),
        ],
        out_specs=[by_head, pl.BlockSpec((length, 2 * HEAD_DIM), lambda i: (0, 0))],
        out_shape=[
            jax.ShapeDtypeStruct((rows, wide), jnp.float32),
            jax.ShapeDtypeStruct((length, 2 * HEAD_DIM), jnp.float32),
        ],
        scratch_shapes=[pltpu.VMEM((rows, length), jnp.bfloat16)],
        compiler_params=pltpu.CompilerParams(vmem_limit_bytes=40 * 2**20),
        cost_estimate=pl.CostEstimate(flops=10**6, bytes_accessed=10**4, transcendentals=0),
    )(probs, grad, query, keys, values)


def body(
    inputs,
    gain_attn,
    w_query,
    w_key,
    w_value,
    w_out,
    gain_moe,
    w_router,
    shared_gate,
    shared_up,
    shared_down,
    expert_gate,
    expert_up,
    expert_down,
    positions,
    routes,
    cotangent,
):
    ctx_count = lax.axis_size("ctx")
    here = lax.axis_index("ctx")
    plane, line, core = ctx_place()
    tok_rows = inputs.shape[1]
    width = inputs.shape[2]
    group = HEADS // KV_HEADS
    scale = HEAD_DIM ** (-0.5)
    experts = w_router.shape[1]
    length = tok_rows * ctx_count
    part_rows = w_query.shape[0]
    capacity = min(tok_rows, 3 * tok_rows * TOP // (2 * experts))
    heads_wide = group * HEAD_DIM
    low = jnp.bfloat16

    narrow = jnp.concatenate([w_router, gain_attn[:, None], gain_moe[:, None]], axis=1)
    narrow = jnp.pad(narrow, ((0, 0), (0, HEAD_DIM - narrow.shape[1])))
    qkv_pack = jnp.concatenate(
        [
            w_query.reshape(part_rows, KV_HEADS, heads_wide),
            w_key.reshape(part_rows, KV_HEADS, HEAD_DIM),
            w_value.reshape(part_rows, KV_HEADS, HEAD_DIM),
            jnp.broadcast_to(narrow[:, None], (part_rows, KV_HEADS, HEAD_DIM)),
            w_out.T.reshape(part_rows, KV_HEADS, heads_wide),
        ],
        axis=2,
    )
    all_routes = gather_small(routes[0].T)
    piece = after(group_slice(qkv_pack), all_routes)
    group_in = gather_group(after(inputs[0], piece)).reshape(CHIP * tok_rows, width)
    peer = peer_block(piece)
    qkv_full = group_weights(piece, peer, group_in)
    hidden_part = shared_gate.shape[1] // ctx_count

    def unit_slices(weight):
        return weight.reshape(part_rows, plane_count(), CHIP, hidden_part)

    shared_pack = jnp.concatenate(
        [unit_slices(shared_gate), unit_slices(shared_up), unit_slices(shared_down.T)], axis=3
    )
    shared_piece = group_slice(
        after(shared_pack.transpose(0, 2, 1, 3).reshape(part_rows, CHIP, -1), piece)
    )
    seq_pos = flip_order(
        positions[0].reshape(plane_count(), LINES, CORES, tok_rows), 1
    ).reshape(length)

    tile_rows = LINES * tok_rows
    tile_slots = LINES * capacity
    tile_count = length // tile_rows
    tile_routes = all_routes.transpose(0, 2, 1).reshape(tile_count, tile_rows, TOP)
    mine = jnp.any(tile_routes == here, axis=2).astype(jnp.int32)
    slot = jnp.where(mine > 0, jnp.cumsum(mine, axis=1) - 1, -1)
    slots = jnp.arange(tile_slots, dtype=jnp.int32)
    place = (slot[:, None, :] == slots[None, :, None]).astype(low)
    place_t = (slot[:, :, None] == slots[None, None, :]).astype(low)
    named = jnp.any(
        tile_routes.reshape(length, TOP, 1) == jnp.arange(128, dtype=jnp.int32), axis=1
    ).astype(jnp.float32)
    own_expert = (jnp.arange(128, dtype=jnp.int32) == here).astype(jnp.float32)[None]
    qkv_full = after(qkv_full, place, place_t, named, peer, shared_piece, group_in)
    qkv_wide = heads_wide + 2 * HEAD_DIM
    qkv_weight = qkv_full[:, :qkv_wide]
    router_wide = qkv_full[:, qkv_wide : qkv_wide + HEAD_DIM]
    out_weight = qkv_full[:, qkv_wide + HEAD_DIM :]
    router_weight = router_wide[:, :experts]
    gain_one = qkv_full[:, qkv_wide + experts].astype(jnp.float32)
    gain_two = qkv_full[:, qkv_wide + experts + 1].astype(jnp.float32)

    wide_in = group_in.astype(jnp.float32)
    inverse_one = lax.rsqrt(jnp.mean(wide_in * wide_in, axis=-1, keepdims=True) + epsilon)
    normed_in = wide_in * inverse_one
    attn_in = (normed_in * gain_one).astype(low)
    group_rows = CHIP * tok_rows
    group_pos = lax.dynamic_slice_in_dim(seq_pos, plane * group_rows, group_rows)
    cosine, sine_table = rope_tables(group_pos, HEAD_DIM)
    qkv = dot32("td,dh->th", attn_in, qkv_weight)
    keys_own = rotate(
        qkv[:, heads_wide : heads_wide + HEAD_DIM][:, None], cosine, sine_table
    )[:, 0].astype(low)
    values_own = qkv[:, heads_wide + HEAD_DIM :].astype(low)
    kv_own = jnp.concatenate([keys_own, values_own], axis=1)
    keys_values = gather_planes(kv_own).reshape(length, 2 * HEAD_DIM)
    gate_half = expert_gate.shape[1] // 2
    gate_first = lax.all_gather(expert_gate[:, :gate_half], "fsdp", axis=1, tiled=True)[0]
    gate_second = lax.all_gather(
        after(expert_gate[:, gate_half:], qkv_full), "fsdp", axis=1, tiled=True
    )[0]
    routed_up = lax.all_gather(after(expert_up, qkv_full), "fsdp", axis=1, tiled=True)[0]
    routed_down = lax.all_gather(after(expert_down, qkv_full), "fsdp", axis=1, tiled=True)[0]
    keys, values = keys_values[:, :HEAD_DIM], keys_values[:, HEAD_DIM:]
    query = (
        rotate(qkv[:, :heads_wide].reshape(group_rows, group, HEAD_DIM), cosine, sine_table)
        .astype(low)
        .reshape(group_rows, heads_wide)
    )
    probs, attended = run_attention(
        query, keys, values, group_pos[:, None], seq_pos[None, :]
    )
    shared_rows = deal_planes(after(shared_piece, kv_own))
    attended = after(attended, shared_rows)
    state_part = dot32("th,dh->td", attended, out_weight).astype(low)
    token_in = inputs[0].astype(jnp.float32)
    state = token_in + scatter_group(state_part.reshape(CORES, LINES, tok_rows, width))

    inverse_two = lax.rsqrt(jnp.mean(state * state, axis=-1, keepdims=True) + epsilon)
    normed_two = state * inverse_two
    moe_in = (normed_two * gain_two).astype(low)
    if lax.axis_size("fsdp") == 2:
        shared_peer = swap(after(shared_rows, attended))
    moe_lines = plane_lines(moe_in)
    all_moe = gather_ctx(moe_lines)
    cot_lines = plane_lines(after(cotangent[0], keys_values))
    all_cot = gather_ctx({k: after(line, moe_in) for k, line in cot_lines.items()})
    if lax.axis_size("fsdp") == 2:
        shared_peer = after(shared_peer, moe_lines[plane_order()[-1]])
        first = lax.axis_index("fsdp") == 0
        shared_weight = jnp.concatenate(
            [
                jnp.where(first, shared_rows, shared_peer),
                jnp.where(first, shared_peer, shared_rows),
            ],
            axis=2,
        ).reshape(width, -1)
    else:
        shared_weight = gather_fsdp(shared_rows, 2).reshape(width, -1)
    shared_parts = [
        shared_weight[:, at * hidden_part : (at + 1) * hidden_part] for at in range(3)
    ]
    (
        moe_keep,
        moe_near,
        out_keep,
        out_near,
        received,
        slot_grad,
        expert_hidden,
        grad_expert_a,
        grad_expert_b,
        shared_hidden,
        grad_shared_a,
        grad_shared_b,
        gates,
    ) = run_experts(
        all_moe,
        all_cot,
        named,
        place,
        place_t,
        own_expert,
        router_wide,
        [gate_first, gate_second, routed_up, routed_down],
        shared_parts,
    )

    sent = {}

    grad_down = outer(expert_hidden, slot_grad)
    sent["down"] = send_fsdp(grad_down, 0)
    moe_keep = after(moe_keep, grad_down)

    def first_work(values):
        held = after(received, *values)
        rows = after(all_moe, *values)
        return outer(held, grad_expert_a), outer(rows, grad_shared_a)

    def second_work(values):
        up = outer(after(received, *values), grad_expert_b)
        sent["gate"] = send_fsdp(works_done[0], 0, sent["down"][1], up)
        sent["up"] = send_fsdp(up, 0, sent["gate"][1])
        return up, sent["gate"][2]

    def third_work(values):
        rows = after(all_moe, *values)
        grad_shared = jnp.concatenate(
            [
                after(works_done[1], *values),
                outer(rows, grad_shared_b),
                outer(after(all_cot, *values), shared_hidden),
            ],
            axis=1,
        )
        sent["shared"] = send_fsdp(
            grad_shared.reshape(ctx_count, -1, 3 * hidden_part), 1, sent["up"][1]
        )
        return (grad_shared,)

    works_done = {}

    def keep_first(values):
        done = first_work(values)
        works_done[0], works_done[1] = done
        return done

    moe_sum, weight_grads, out_rows = scatter_two(
        (moe_keep, moe_near),
        (out_keep, out_near),
        [keep_first, second_work, third_work],
        lambda: [sent["gate"][1]],
    )
    out_steps = out_rows(moe_sum)
    out_moved = [next(out_steps)]
    for unused in plane_order()[1:]:
        out_moved.append(out_steps.send(moe_sum))
    grad_moe_sum = moe_sum[:, :width]
    grad_gates = moe_sum[:, width : width + experts].T

    home_gates = gates[:tok_rows, :experts].T
    gate_mean = jnp.sum(home_gates * grad_gates, axis=0, keepdims=True)
    grad_logits = home_gates * (grad_gates - gate_mean)
    grad_router = jnp.einsum(
        "td,et->de", moe_in.astype(jnp.float32), grad_logits, precision=highest
    )
    grad_moe_in = grad_moe_sum + jnp.einsum(
        "et,de->td", grad_logits, router_weight.astype(jnp.float32), precision=highest
    )
    grad_gain_two, grad_through = norm_back(grad_moe_in, normed_two, inverse_two, gain_two)
    grad_state = cotangent[0].astype(jnp.float32) + grad_through
    group_proj = gather_group(grad_state.astype(low)).reshape(group_rows, width)
    grad_expert_down = add_fsdp(*sent["down"])
    group_proj, grad_expert_down = together(group_proj, grad_expert_down)

    grad_attended = dot32("td,dh->th", group_proj, out_weight).astype(low)
    grad_query_rot, grad_kv_part = run_attention_back(probs, grad_attended, query, keys, values)
    grad_query_rot = grad_query_rot.reshape(group_rows, group, HEAD_DIM)
    grad_expert_gate = add_fsdp(*sent["gate"])
    grad_kv_part, *unused = together(grad_kv_part, *out_moved, sent["up"][1])
    up_arrived = sent["up"][1]
    grad_kv_part = grad_kv_part.reshape(plane_count(), group_rows, 2 * HEAD_DIM)
    kv_away = planes_away(grad_kv_part)
    grad_keys_values = scatter_planes(grad_kv_part, away=kv_away)
    grad_expert_up = add_fsdp(sent["up"][0], up_arrived)
    grad_query_pre = (
        rotate(grad_query_rot, cosine, -sine_table).astype(low).reshape(group_rows, heads_wide)
    )
    query_sent = send_grads(
        dot32("td,th->dh", attn_in, grad_query_pre), sent["shared"][1]
    )
    grad_keys_values, grad_expert_gate, *unused = together(
        grad_keys_values, grad_expert_gate, sent["shared"][1]
    )
    grad_keys_pre = rotate(grad_keys_values[:, None, :HEAD_DIM], cosine, -sine_table)[:, 0]
    grad_kv_pre = jnp.concatenate(
        [grad_keys_pre.astype(low), grad_keys_values[:, HEAD_DIM:].astype(low)], axis=1
    )
    attn_part = dot32("th,dh->td", grad_query_pre, qkv_weight[:, :heads_wide]) + dot32(
        "th,dh->td", grad_kv_pre, qkv_weight[:, heads_wide:]
    )
    grad_attn_in = scatter_group(attn_part.astype(low).reshape(CORES, LINES, tok_rows, width))
    grad_gain_one = jnp.sum(attn_part * normed_in, axis=0)
    grad_kv = jnp.concatenate(
        [
            dot32("td,th->dh", attn_in, grad_kv_pre),
            grad_gain_one[:, None],
            grad_gain_two[:, None],
            jnp.pad(grad_router, ((0, 0), (0, HEAD_DIM - 2 - experts))),
        ],
        axis=1,
    )
    shared_back = collected(*sent["shared"][:2], low)
    grad_attn_in, query_arrived = together(grad_attn_in, query_sent[1])
    grad_kv = after(grad_kv, grad_attn_in)
    kv_sent = send_grads(grad_kv, query_arrived)
    query_planes = scatter_planes(
        plane_view(add_fsdp(query_sent[0], after(query_arrived, kv_sent[2])))
    )
    back_gate = shared_back[:, :, :hidden_part].reshape(part_rows, -1)
    back_up = shared_back[:, :, hidden_part : 2 * hidden_part].reshape(part_rows, -1)
    back_down = shared_back[:, :, 2 * hidden_part :].reshape(part_rows, -1).T
    output = (state + out_steps.send(grad_keys_values)).astype(low)
    kv_arrived = after(kv_sent[1], back_gate, back_up, back_down, output, grad_expert_up)
    kv_total = plane_view(add_fsdp(kv_sent[0], kv_arrived))
    out_own, out_arrived = planes_sent(
        grads_view(dot32("td,th->dh", group_proj, after(attended, *kv_away.values())))
    )
    kv_total, out_own = together(kv_total, out_own)
    kv_planes = scatter_planes(kv_total)
    out_planes = planes_total(out_own, out_arrived)
    planes_sum = jnp.concatenate(
        [query_planes, scatter_fsdp(out_planes, 1)[:, 0], kv_planes], axis=2
    )
    planes_sum, grad_attn_in, back_gate, back_up, back_down, output = together(
        planes_sum, grad_attn_in, back_gate, back_up, back_down, output
    )
    all_back = undeal_group(
        planes_sum.astype(low).reshape(LINES, CORES, part_rows, planes_sum.shape[2])
    )
    all_back = all_back.reshape(part_rows, CHIP, -1).astype(jnp.float32)
    query_back = all_back[:, :, :heads_wide]
    out_back = all_back[:, :, heads_wide : 2 * heads_wide]
    kv_back = all_back[:, :, 2 * heads_wide :]
    narrow_back = jnp.sum(kv_back[:, :, 2 * HEAD_DIM :], axis=1)
    home_inverse = lax.rsqrt(jnp.mean(token_in * token_in, axis=-1, keepdims=True) + epsilon)
    unused, grad_first = norm_back(grad_attn_in, token_in * home_inverse, home_inverse, gain_one)
    grad_inputs = (grad_state + grad_first).astype(low)

    return (
        output[None],
        grad_inputs[None],
        narrow_back[:, 0],
        query_back.reshape(part_rows, -1),
        kv_back[:, :, :HEAD_DIM].reshape(part_rows, -1),
        kv_back[:, :, HEAD_DIM : 2 * HEAD_DIM].reshape(part_rows, -1),
        out_back.reshape(part_rows, -1).T,
        narrow_back[:, 1],
        narrow_back[:, 2 : 2 + experts],
        back_gate,
        back_up,
        back_down,
        grad_expert_gate[None],
        grad_expert_up[None],
        grad_expert_down[None],
    )


def solution(mesh):
    in_specs = (
        P("fsdp", "ctx", None),
        P(("ctx", "fsdp")),
        P(("ctx", "fsdp"), None),
        P(("ctx", "fsdp"), None),
        P(("ctx", "fsdp"), None),
        P(None, ("ctx", "fsdp")),
        P(("ctx", "fsdp")),
        P(("ctx", "fsdp"), None),
        P(("ctx", "fsdp"), None),
        P(("ctx", "fsdp"), None),
        P(None, ("ctx", "fsdp")),
        P("ctx", "fsdp", None),
        P("ctx", "fsdp", None),
        P("ctx", "fsdp", None),
        P("fsdp", None),
        P("fsdp", "ctx", None),
        P("fsdp", "ctx", None),
    )
    out_specs = (
        P("fsdp", "ctx", None),
        P("fsdp", "ctx", None),
        P(("ctx", "fsdp")),
        P(("ctx", "fsdp"), None),
        P(("ctx", "fsdp"), None),
        P(("ctx", "fsdp"), None),
        P(None, ("ctx", "fsdp")),
        P(("ctx", "fsdp")),
        P(("ctx", "fsdp"), None),
        P(("ctx", "fsdp"), None),
        P(("ctx", "fsdp"), None),
        P(None, ("ctx", "fsdp")),
        P("ctx", "fsdp", None),
        P("ctx", "fsdp", None),
        P("ctx", "fsdp", None),
    )
    return jax.shard_map(body, mesh=mesh, in_specs=in_specs, out_specs=out_specs, check_vma=False)
```

```python
import functools

import jax
import jax.numpy as jnp
from jax import lax
from jax.experimental import pallas as pl
from jax.experimental.pallas import tpu as pltpu
from jax.sharding import PartitionSpec as P

HEADS = 16
KV_HEADS = 4
HEAD_DIM = 128
TOP = 6


epsilon = 1e-06
rope_base = 600000.0
highest = lax.Precision.HIGHEST


def rope_tables(position_row, head_size):
    half_size = head_size // 2
    freq_steps = jnp.arange(half_size, dtype=jnp.float32)
    frequency = rope_base ** (-(freq_steps / half_size))
    angles = position_row.astype(jnp.float32)[:, None] * frequency[None, :]
    return (jnp.cos(angles), jnp.sin(angles))


def rotate(values, cosine, sine_table):
    half_size = values.shape[-1] // 2
    first_half = values[..., :half_size]
    second_half = values[..., half_size:]
    cosine_wide = cosine[:, None, :]
    sine_wide = sine_table[:, None, :]
    return jnp.concatenate(
        [
            first_half * cosine_wide - second_half * sine_wide,
            second_half * cosine_wide + first_half * sine_wide,
        ],
        axis=-1,
    )


def silu_slope(values):
    sigmoid_part = lax.logistic(values)
    return sigmoid_part * (1.0 + values * (1.0 - sigmoid_part))


def norm_back(grad_normed, normed, inverse, gain):
    grad_gain = jnp.sum(grad_normed * normed, axis=0)
    scaled = grad_normed * gain
    grad_values = inverse * (scaled - normed * jnp.mean(scaled * normed, axis=-1, keepdims=True))
    return (grad_gain, grad_values)


CORES = 2
LINES = 2
CHIP = CORES * LINES


def ctx_place():
    here = lax.axis_index("ctx")
    return here // CHIP, here // CORES % LINES, here % CORES


def plane_count():
    return lax.axis_size("ctx") // CHIP


def plane_order():
    planes = plane_count()
    return sorted(range(1, planes), key=lambda k: (min(k, planes - k), k))


def shift(values, step):
    planes = plane_count()
    pairs = [
        (i, (i // CHIP + step) % planes * CHIP + i % CHIP) for i in range(lax.axis_size("ctx"))
    ]
    return lax.ppermute(values, "ctx", pairs)


def flip(values, bit):
    return lax.ppermute(values, "ctx", [(i, i ^ bit) for i in range(lax.axis_size("ctx"))])


def swap(values):
    return lax.ppermute(values, "fsdp", [(0, 1), (1, 0)])


def part(values, index, axis=0):
    return lax.dynamic_index_in_dim(values, index, axis, keepdims=False)


def pair(mine, other, place, axis):
    first = place == 0
    return jnp.stack(
        [jnp.where(first, mine, other), jnp.where(first, other, mine)], axis=axis
    )


def after(values, *others):
    return lax.optimization_barrier((values, *others))[0]


def together(*values):
    return lax.optimization_barrier(values)


def gather_group(block):
    across = flip(block, CORES)
    return jnp.stack([block, across, flip(block, 1), flip(across, 1)])


def scatter_group(partial):
    near = flip(partial[1], 1)
    chip = partial[0].astype(jnp.float32) + near.astype(jnp.float32)
    across = flip(chip[1].astype(jnp.bfloat16), CORES)
    return chip[0] + across.astype(jnp.float32)


def flip_order(values, axis):
    z, y, c = ctx_place()
    lines = jnp.where(y == 0, values, jnp.flip(values, axis))
    cores = jnp.where(c == 0, lines, jnp.flip(lines, axis + 1))
    return jnp.swapaxes(cores, axis, axis + 1)


def gather_planes(piece):
    z, y, c = ctx_place()
    planes = plane_count()
    found = jnp.zeros((planes,) + piece.shape, piece.dtype)
    for k in [0] + plane_order():
        moved = shift(piece, k) if k else piece
        found = lax.dynamic_update_slice(
            found, moved[None], ((z - k) % planes,) + (0,) * piece.ndim
        )
    return found


def planes_away(partial):
    z, y, c = ctx_place()
    planes = plane_count()
    return {k: part(partial, (z - k) % planes).astype(jnp.bfloat16) for k in plane_order()}


def planes_total(own, arrived):
    for values in arrived:
        own = own + values.astype(jnp.float32)
    return own


def planes_sent(partial, away=None):
    away = planes_away(partial) if away is None else away
    return part(partial, ctx_place()[0]), [shift(away[k], -k) for k in plane_order()]


def scatter_planes(partial, away=None):
    return planes_total(*planes_sent(partial, away))


def plane_lines(block):
    return {k: shift(block, k) if k else block for k in [0] + plane_order()}


def gather_ctx(lines):
    planes = plane_count()
    found = {}
    for k in [0] + plane_order():
        chips = (lines[k], flip(lines[k], CORES))
        found[k] = chips + tuple(flip(piece, 1) for piece in chips)
    return jnp.concatenate([piece for k in range(planes) for piece in found[k]], axis=0)


def chip_step(keep, near, order, *first):
    planes = plane_count()
    near = flip(after(near, *first), 1)
    shape = (planes, LINES, keep.shape[0] // (planes * LINES), keep.shape[1])
    keep, near = keep.reshape(shape), near.reshape(shape)
    kept, sent, arrived = {}, {}, {}
    for k in order:
        kept[k] = keep[k, 0].astype(jnp.float32) + near[k, 0].astype(jnp.float32)
        chip = keep[k, 1].astype(jnp.float32) + near[k, 1].astype(jnp.float32)
        sent[k] = chip.astype(jnp.bfloat16)
        arrived[k] = flip(sent[k], CORES)
    return kept, sent, arrived


def scatter_two(partial, other, works, last):
    order = plane_order()[::-1] + [0]
    kept, sent, arrived = chip_step(*partial, order)
    other_kept, other_sent, other_arrived = chip_step(*other, order, *[sent[k] for k in order])
    results = [works[0]([sent[k] for k in order] + [other_sent[k] for k in order])]
    total, moved = None, ()
    for step, k in enumerate(order):
        ready = [other_arrived[order[step - 2]]] if step > 1 else []
        if not k:
            ready = ready + last()
        line = after(kept[k], *moved, *results[-1], *ready) + arrived[k].astype(jnp.float32)
        if k:
            away = line.astype(jnp.bfloat16)
            moved = (shift(away, -k),)
            line = moved[0].astype(jnp.float32)
            if step + 1 < len(works):
                results.append(works[step + 1]([away]))
        total = line if total is None else total + line

    def other_rows(reached):
        total = None
        for k in order:
            line = after(other_kept[k], reached) + other_arrived[k].astype(jnp.float32)
            if k:
                moved = shift(line.astype(jnp.bfloat16), -k)
                reached = yield moved
                line = moved.astype(jnp.float32)
            total = line if total is None else total + line
        yield total

    return total, [value for result in results for value in result], other_rows


def gather_small(values):
    both = jnp.stack([values, flip(values, 1)])
    plane = jnp.stack([both, flip(both, CORES)], axis=1)
    found = {0: plane}
    for k in plane_order():
        found[k] = shift(plane, k)
    return jnp.stack([found[k] for k in range(plane_count())]).reshape((-1,) + values.shape)


def peer_block(block):
    return swap(block) if lax.axis_size("fsdp") == 2 else gather_fsdp(block, 1)


def gather_fsdp(block, axis):
    if lax.axis_size("fsdp") != 2:
        return lax.all_gather(block, "fsdp", axis=axis, tiled=True)
    peer = swap(block)
    first = lax.axis_index("fsdp") == 0
    return jnp.concatenate(
        [jnp.where(first, block, peer), jnp.where(first, peer, block)], axis=axis
    )


def send_fsdp(total, axis, *first):
    if lax.axis_size("fsdp") != 2:
        away = after(total.astype(jnp.bfloat16), *first)
        return None, lax.psum_scatter(away, "fsdp", scatter_dimension=axis, tiled=True), away
    here = lax.axis_index("fsdp")
    half = total.shape[axis] // 2
    away = lax.dynamic_slice_in_dim(total, (1 - here) * half, half, axis)
    kept = lax.dynamic_slice_in_dim(total, here * half, half, axis)
    away = away.astype(jnp.bfloat16)
    return kept, swap(after(away, *first)), away


def add_fsdp(kept, arrived, away=None):
    arrived = arrived.astype(jnp.float32)
    return arrived if kept is None else kept.astype(jnp.float32) + arrived


def scatter_fsdp(total, axis):
    return add_fsdp(*send_fsdp(total, axis)[:2])


def deal_group(pack):
    z, y, c = ctx_place()
    lines = pair(part(pack, y, 1), flip(part(pack, 1 - y, 1), CORES), y, 0)
    return pair(part(lines, c, 2), flip(part(lines, 1 - c, 2), 1), c, 1)


def undeal_group(slices):
    z, y, c = ctx_place()
    cores = pair(part(slices, c, 1), flip(part(slices, 1 - c, 1), 1), c, 2)
    return pair(part(cores, y), flip(part(cores, 1 - y), CORES), y, 1)


def group_slice(pack):
    rows, count, size = pack.shape
    return deal_group(pack.reshape(rows, LINES, CORES, size)).reshape(CHIP, 1, rows, size)


def deal_planes(piece):
    z, y, c = ctx_place()
    planes = plane_count()
    size = piece.shape[-1] // planes
    found = jnp.zeros((planes,) + piece.shape[:-1] + (size,), piece.dtype)
    for k in [0] + plane_order():
        away = lax.dynamic_slice_in_dim(piece, (z + k) % planes * size, size, piece.ndim - 1)
        moved = shift(away, k) if k else away
        found = lax.dynamic_update_slice(
            found, moved[None], ((z - k) % planes,) + (0,) * piece.ndim
        )
    return found


def group_weights(piece, peer, *first):
    z, y, c = ctx_place()
    planes, shards = plane_count(), lax.axis_size("fsdp")
    rows, size = piece.shape[2:]
    if shards != 2:
        return gather_planes(gather_fsdp(piece, 1)).reshape(-1, size)
    x = lax.axis_index("fsdp")
    found = jnp.zeros((planes, CHIP, shards, rows, size), piece.dtype)
    for k in [0] + plane_order():
        moved = shift(piece, k) if k else piece
        other = swap(after(moved, other)) if k else after(peer, *first)
        for side, block in ((x, moved), (1 - x, other)):
            found = lax.dynamic_update_slice(
                found, block[None], ((z - k) % planes, 0, side, 0, 0)
            )
    return found.reshape(-1, size)


def send_grads(grad, *first):
    planes, shards = plane_count(), lax.axis_size("fsdp")
    rows = grad.shape[0] // (planes * CHIP * shards)
    return send_fsdp(grad.reshape(planes, CHIP, shards, rows, grad.shape[1]), 2, *first)


def grads_view(grad):
    planes, shards = plane_count(), lax.axis_size("fsdp")
    rows = grad.shape[0] // (planes * CHIP * shards)
    return grad.reshape(planes, CHIP, shards, rows, grad.shape[1])


def plane_view(total):
    planes, place, shards, rows, size = total.shape
    return total.reshape(planes, place, rows, size)


def sum_fsdp(total):
    return lax.psum_scatter(
        total.astype(jnp.bfloat16), "fsdp", scatter_dimension=0, tiled=True
    ).astype(jnp.float32)


def collected(kept, arrived, kind):
    moved = lax.all_to_all(
        add_fsdp(kept, arrived).astype(kind), "ctx", split_axis=0, concat_axis=0, tiled=True
    )
    return moved.astype(jnp.float32).transpose(1, 0, 2)


def dot32(spec, left, right):
    return jnp.einsum(spec, left, right, preferred_element_type=jnp.float32)


def chunks_of(size, step):
    return [(at, min(step, size - at)) for at in range(0, size, step)]


def dot_nt(left, right):
    return lax.dot_general(
        left, right, (((1,), (1,)), ((), ())), preferred_element_type=jnp.float32
    )


def dot_nn(left, right):
    return jnp.dot(left, right, preferred_element_type=jnp.float32)


def dot_tn(left, right):
    return lax.dot_general(
        left, right, (((0,), (0,)), ((), ())), preferred_element_type=jnp.float32
    )


def silu_parts(values):
    sigmoid_part = 0.5 + 0.5 * jnp.tanh(0.5 * values)
    return values * sigmoid_part, sigmoid_part * (1.0 + values * (1.0 - sigmoid_part))


def experts_kernel(
    piece,
    tok, cot, named, place, place_t, mine, router, far_gate, far_late, far_up, far_down, s_gate, s_up, s_down,
    moe_keep, moe_near, out_keep, out_near, received, slot_grad, hidden, grad_a, grad_b, shared_hidden, grad_sa,
    grad_sb, gates, slot_cot,
    w_gate, w_gate_late, w_up, w_down, arrived,
):
    low = jnp.bfloat16
    width, units = tok.shape[1], w_gate.shape[1]
    copies = [
        pltpu.make_async_copy(far, near, arrived.at[j])
        for j, (far, near) in enumerate(
            ((far_gate, w_gate), (far_late, w_gate_late), (far_up, w_up), (far_down, w_down))
        )
    ]

    @pl.when(pl.program_id(0) == 0)
    def _():
        for copy in copies:
            copy.start()

    half, rows = tok.shape[0] // 2, place.shape[1]
    low_rows, high_rows = slice(0, rows), slice(rows, 2 * rows)
    halves = ((slice(0, half), low_rows), (slice(half, 2 * half), high_rows))
    gates_in = (w_gate, w_gate_late)
    logits = dot_nn(tok[...], router[...])
    chosen = named[...] > 0
    peak = jnp.max(jnp.where(chosen, logits, -1e30), axis=1, keepdims=True)
    raised = jnp.where(chosen, jnp.exp(jnp.where(chosen, logits - peak, 0.0)), 0.0)
    shares = raised / jnp.sum(raised, axis=1, keepdims=True)
    gates[...] = shares
    own = [
        jnp.dot(
            place[h].astype(jnp.float32),
            (shares * mine[...])[toks],
            precision=highest,
            preferred_element_type=jnp.float32,
        )
        for h, (toks, picks) in enumerate(halves)
    ]
    slot_gate = jnp.sum(jnp.concatenate(own, axis=0), axis=1, keepdims=True)

    step = 256
    for at, size in chunks_of(width, step):
        for h, (toks, picks) in enumerate(halves):
            received[picks, at : at + size] = dot_nn(place[h], tok[toks, at : at + size]).astype(low)
            found = dot_nn(place[h], cot[toks, at : at + size])
            slot_cot[picks, at : at + size] = found.astype(low)
            slot_grad[picks, at : at + size] = (slot_gate[picks] * found).astype(low)

    shared_a = dot_nn(tok[...], s_gate[...])
    shared_b = dot_nn(tok[...], s_up[...])
    act, slope = silu_parts(shared_a)
    shared_hidden[...] = (act * shared_b).astype(low)
    grad_sh = dot_nn(cot[...], s_down[...])
    grad_sa[...] = (grad_sh * shared_b * slope).astype(low)
    grad_sb[...] = (grad_sh * act).astype(low)

    @pl.when(pl.program_id(0) == 0)
    def _():
        for copy in copies:
            copy.wait()

    def unit_step(at, size):
        value_a = 0.0
        for j in range(width // piece):
            rows = slice(j // 2 * piece, (j // 2 + 1) * piece)
            value_a = value_a + dot_nn(
                received[:, j * piece : (j + 1) * piece], gates_in[j % 2][rows, pl.ds(at, size)]
            )
        value_b = dot_nn(received[...], w_up[:, pl.ds(at, size)])
        act, slope = silu_parts(value_a)
        hidden[:, pl.ds(at, size)] = (act * value_b).astype(low)
        grad_h = dot_nt(slot_grad[...], w_down[pl.ds(at, size), :])
        grad_a[:, pl.ds(at, size)] = (grad_h * value_b * slope).astype(low)
        grad_b[:, pl.ds(at, size)] = (grad_h * act).astype(low)

    for at, size in chunks_of(units, 1408):
        unit_step(at, size)

    step = piece

    def width_loop(i, score):
        at = i * step
        here = pl.ds(at, step)
        gate_rows = gates_in[i % 2][i // 2 * step : (i // 2 + 1) * step, :]
        row = dot_nt(grad_a[...], gate_rows) + dot_nt(grad_b[...], w_up[here, :])
        row = row.astype(low)
        for h, (toks, picks) in enumerate(halves):
            (moe_keep, moe_near)[h][:, here] = (
                dot_nn(place_t[h], row[picks])
                + dot_nt(grad_sa[toks, :], s_gate[here, :])
                + dot_nt(grad_sb[toks, :], s_up[here, :])
            ).astype(low)
        made = dot_nn(hidden[...], w_down[:, here]).astype(low).astype(jnp.float32)
        row = (slot_gate * made).astype(low)
        for h, (toks, picks) in enumerate(halves):
            (out_keep, out_near)[h][:, here] = (
                dot_nn(place_t[h], row[picks]) + dot_nt(shared_hidden[toks, :], s_down[here, :])
            ).astype(low)
        return score + jnp.sum(slot_cot[:, here].astype(jnp.float32) * made, axis=1, keepdims=True)

    score = jnp.zeros((received.shape[0], 1), jnp.float32)
    for i in range(width // step):
        score = width_loop(i, score)
    for h, (toks, picks) in enumerate(halves):
        (moe_keep, moe_near)[h][:, width:] = jnp.dot(
            place_t[h].astype(jnp.float32),
            score[picks] * mine[...],
            precision=highest,
            preferred_element_type=jnp.float32,
        ).astype(low)


def run_experts(tok, cot, named, place, place_t, mine, router, weights, shared):
    count, slots, tile = place.shape[0] // 2, 2 * place.shape[1], 2 * place.shape[2]
    width = tok.shape[1]
    units, share = weights[0].shape[1], shared[0].shape[1]
    low = jnp.bfloat16

    def tiles(size, columns):
        return pl.BlockSpec((size, columns), lambda i: (i, 0))

    def whole(array):
        return pl.BlockSpec(
            array.shape, lambda i: (0,) * array.ndim, pipeline_mode=pl.Buffered(1)
        )

    outs = [
        (tile // 2, width + 128, low),
        (tile // 2, width + 128, low),
        (tile // 2, width, low),
        (tile // 2, width, low),
        (slots, width, low),
        (slots, width, low),
        (slots, units, low),
        (slots, units, low),
        (slots, units, low),
        (tile, share, low),
        (tile, share, low),
        (tile, share, low),
        (tile, 128, jnp.float32),
    ]
    piece = weights[0].shape[0] // lax.axis_size("fsdp")
    return pl.pallas_call(
        functools.partial(experts_kernel, piece),
        grid=(count,),
        in_specs=[
            tiles(tile, width),
            tiles(tile, width),
            tiles(tile, 128),
            pl.BlockSpec((2,) + place.shape[1:], lambda i: (i, 0, 0)),
            pl.BlockSpec((2,) + place_t.shape[1:], lambda i: (i, 0, 0)),
            whole(mine),
            whole(router),
        ]
        + [pl.BlockSpec(memory_space=pl.ANY) for w in weights]
        + [whole(w) for w in shared],
        out_specs=[tiles(size, columns) for size, columns, kind in outs],
        out_shape=[
            jax.ShapeDtypeStruct((count * size, columns), kind) for size, columns, kind in outs
        ],
        scratch_shapes=[pltpu.VMEM((slots, width), low)]
        + [pltpu.VMEM(w.shape, low) for w in weights]
        + [pltpu.SemaphoreType.DMA((len(weights),))],
        compiler_params=pltpu.CompilerParams(vmem_limit_bytes=60 * 2**20),
        cost_estimate=pl.CostEstimate(flops=10**10, bytes_accessed=10**7, transcendentals=0),
    )(tok, cot, named, place, place_t, mine, router, *weights, *shared)


def outer_kernel(left, right, out):
    for at, size in chunks_of(right.shape[1], 256):
        out[:, at : at + size] = dot_tn(left[...], right[:, at : at + size]).astype(out.dtype)


def outer(left, right, kind=jnp.bfloat16):
    rows, height = left.shape
    columns = right.shape[1]
    tile = 256 if height % 256 == 0 else 128
    return pl.pallas_call(
        outer_kernel,
        grid=(height // tile,),
        in_specs=[
            pl.BlockSpec((rows, tile), lambda i: (0, i)),
            pl.BlockSpec((rows, columns), lambda i: (0, 0), pipeline_mode=pl.Buffered(1)),
        ],
        out_specs=pl.BlockSpec((tile, columns), lambda i: (i, 0)),
        out_shape=jax.ShapeDtypeStruct((height, columns), kind),
        compiler_params=pltpu.CompilerParams(vmem_limit_bytes=40 * 2**20),
        cost_estimate=pl.CostEstimate(flops=10**6, bytes_accessed=10**4, transcendentals=0),
    )(left, right)


def attention_kernel(query, keys, values, own_pos, seq_pos, probs, attended):
    scale = HEAD_DIM ** (-0.5)
    rows = query.shape[0]
    step = 128
    for at in range(0, rows, step):
        here = slice(at, at + step)
        scores = dot_nt(query[here, :], keys[...]) * scale
        scores = jnp.where(own_pos[here, :] >= seq_pos[...], scores, -1e30)
        raised = jnp.exp(scores - jnp.max(scores, axis=1, keepdims=True))
        share = (raised * (1.0 / jnp.sum(raised, axis=1, keepdims=True))).astype(jnp.bfloat16)
        probs[here, :] = share
        attended[here, :] = dot_nn(share, values[...]).astype(jnp.bfloat16)


def run_attention(query, keys, values, own_pos, seq_pos):
    rows, wide = query.shape
    heads, length = wide // HEAD_DIM, keys.shape[0]

    def whole(array):
        return pl.BlockSpec(array.shape, lambda i: (0, 0))

    by_head = pl.BlockSpec((rows, HEAD_DIM), lambda i: (0, i))
    return pl.pallas_call(
        attention_kernel,
        grid=(heads,),
        in_specs=[by_head, whole(keys), whole(values), whole(own_pos), whole(seq_pos)],
        out_specs=[pl.BlockSpec((None, rows, length), lambda i: (i, 0, 0)), by_head],
        out_shape=[
            jax.ShapeDtypeStruct((heads, rows, length), jnp.bfloat16),
            jax.ShapeDtypeStruct((rows, wide), jnp.bfloat16),
        ],
        compiler_params=pltpu.CompilerParams(vmem_limit_bytes=40 * 2**20),
        cost_estimate=pl.CostEstimate(flops=10**6, bytes_accessed=10**4, transcendentals=0),
    )(query, keys, values, own_pos, seq_pos)


def attention_back_kernel(probs, grad, query, keys, values, grad_query, grad_both, grad_scores):
    scale = HEAD_DIM ** (-0.5)
    rows = query.shape[0]
    step = 128
    for at in range(0, rows, step):
        here = slice(at, at + step)
        grad_probs = dot_nt(grad[here, :], values[...])
        share = probs[here, :].astype(jnp.float32)
        row_dot = jnp.sum(share * grad_probs, axis=1, keepdims=True)
        low_scores = (share * (grad_probs - row_dot)).astype(jnp.bfloat16)
        grad_scores[here, :] = low_scores
        grad_query[here, :] = dot_nn(low_scores, keys[...]) * scale

    def add(part, value):
        @pl.when(pl.program_id(0) == 0)
        def _():
            grad_both[:, part] = value

        @pl.when(pl.program_id(0) != 0)
        def _():
            grad_both[:, part] += value

    add(slice(0, HEAD_DIM), dot_tn(grad_scores[...], query[...]) * scale)
    add(slice(HEAD_DIM, 2 * HEAD_DIM), dot_tn(probs[...], grad[...]))


def run_attention_back(probs, grad, query, keys, values):
    rows, wide = query.shape
    heads, length = wide // HEAD_DIM, keys.shape[0]

    def whole(array):
        return pl.BlockSpec(array.shape, lambda i: (0, 0))

    by_head = pl.BlockSpec((rows, HEAD_DIM), lambda i: (0, i))
    return pl.pallas_call(
        attention_back_kernel,
        grid=(heads,),
        in_specs=[
            pl.BlockSpec((None, rows, length), lambda i: (i, 0, 0)),
            by_head,
            by_head,
            whole(keys),
            whole(values),
        ],
        out_specs=[by_head, pl.BlockSpec((length, 2 * HEAD_DIM), lambda i: (0, 0))],
        out_shape=[
            jax.ShapeDtypeStruct((rows, wide), jnp.float32),
            jax.ShapeDtypeStruct((length, 2 * HEAD_DIM), jnp.float32),
        ],
        scratch_shapes=[pltpu.VMEM((rows, length), jnp.bfloat16)],
        compiler_params=pltpu.CompilerParams(vmem_limit_bytes=40 * 2**20),
        cost_estimate=pl.CostEstimate(flops=10**6, bytes_accessed=10**4, transcendentals=0),
    )(probs, grad, query, keys, values)


def body(
    inputs,
    gain_attn,
    w_query,
    w_key,
    w_value,
    w_out,
    gain_moe,
    w_router,
    shared_gate,
    shared_up,
    shared_down,
    expert_gate,
    expert_up,
    expert_down,
    positions,
    routes,
    cotangent,
):
    ctx_count = lax.axis_size("ctx")
    here = lax.axis_index("ctx")
    plane, line, core = ctx_place()
    tok_rows = inputs.shape[1]
    width = inputs.shape[2]
    group = HEADS // KV_HEADS
    scale = HEAD_DIM ** (-0.5)
    experts = w_router.shape[1]
    length = tok_rows * ctx_count
    part_rows = w_query.shape[0]
    capacity = min(tok_rows, 3 * tok_rows * TOP // (2 * experts))
    heads_wide = group * HEAD_DIM
    low = jnp.bfloat16

    narrow = jnp.concatenate([w_router, gain_attn[:, None], gain_moe[:, None]], axis=1)
    narrow = jnp.pad(narrow, ((0, 0), (0, HEAD_DIM - narrow.shape[1])))
    qkv_pack = jnp.concatenate(
        [
            w_query.reshape(part_rows, KV_HEADS, heads_wide),
            w_key.reshape(part_rows, KV_HEADS, HEAD_DIM),
            w_value.reshape(part_rows, KV_HEADS, HEAD_DIM),
            jnp.broadcast_to(narrow[:, None], (part_rows, KV_HEADS, HEAD_DIM)),
            w_out.T.reshape(part_rows, KV_HEADS, heads_wide),
        ],
        axis=2,
    )
    all_routes = gather_small(routes[0].T)
    piece = after(group_slice(qkv_pack), all_routes)
    group_in = gather_group(after(inputs[0], piece)).reshape(CHIP * tok_rows, width)
    peer = peer_block(piece)
    qkv_full = group_weights(piece, peer, group_in)
    hidden_part = shared_gate.shape[1] // ctx_count

    def unit_slices(weight):
        return weight.reshape(part_rows, plane_count(), CHIP, hidden_part)

    shared_pack = jnp.concatenate(
        [unit_slices(shared_gate), unit_slices(shared_up), unit_slices(shared_down.T)], axis=3
    )
    shared_piece = group_slice(
        after(shared_pack.transpose(0, 2, 1, 3).reshape(part_rows, CHIP, -1), piece)
    )
    seq_pos = flip_order(
        positions[0].reshape(plane_count(), LINES, CORES, tok_rows), 1
    ).reshape(length)

    tile_rows = LINES * tok_rows
    tile_slots = LINES * capacity
    tile_count = length // tile_rows
    tile_routes = all_routes.transpose(0, 2, 1).reshape(tile_count, tile_rows, TOP)
    mine = jnp.any(tile_routes == here, axis=2).astype(jnp.int32)
    slot = jnp.where(mine > 0, jnp.cumsum(mine, axis=1) - 1, -1)
    slots = jnp.arange(tile_slots, dtype=jnp.int32)
    place = (slot[:, None, :] == slots[None, :, None]).astype(low)
    place_t = (slot[:, :, None] == slots[None, None, :]).astype(low)
    named = jnp.any(
        tile_routes.reshape(length, TOP, 1) == jnp.arange(128, dtype=jnp.int32), axis=1
    ).astype(jnp.float32)
    own_expert = (jnp.arange(128, dtype=jnp.int32) == here).astype(jnp.float32)[None]
    qkv_full = after(qkv_full, place, place_t, named, peer, shared_piece, group_in)
    qkv_wide = heads_wide + 2 * HEAD_DIM
    qkv_weight = qkv_full[:, :qkv_wide]
    router_wide = qkv_full[:, qkv_wide : qkv_wide + HEAD_DIM]
    out_weight = qkv_full[:, qkv_wide + HEAD_DIM :]
    router_weight = router_wide[:, :experts]
    gain_one = qkv_full[:, qkv_wide + experts].astype(jnp.float32)
    gain_two = qkv_full[:, qkv_wide + experts + 1].astype(jnp.float32)

    wide_in = group_in.astype(jnp.float32)
    inverse_one = lax.rsqrt(jnp.mean(wide_in * wide_in, axis=-1, keepdims=True) + epsilon)
    normed_in = wide_in * inverse_one
    attn_in = (normed_in * gain_one).astype(low)
    group_rows = CHIP * tok_rows
    group_pos = lax.dynamic_slice_in_dim(seq_pos, plane * group_rows, group_rows)
    cosine, sine_table = rope_tables(group_pos, HEAD_DIM)
    qkv = dot32("td,dh->th", attn_in, qkv_weight)
    keys_own = rotate(
        qkv[:, heads_wide : heads_wide + HEAD_DIM][:, None], cosine, sine_table
    )[:, 0].astype(low)
    values_own = qkv[:, heads_wide + HEAD_DIM :].astype(low)
    kv_own = jnp.concatenate([keys_own, values_own], axis=1)
    keys_values = gather_planes(kv_own).reshape(length, 2 * HEAD_DIM)
    gate_half = expert_gate.shape[1] // 2
    gate_first = lax.all_gather(expert_gate[:, :gate_half], "fsdp", axis=1, tiled=True)[0]
    gate_second = lax.all_gather(
        after(expert_gate[:, gate_half:], qkv_full), "fsdp", axis=1, tiled=True
    )[0]
    routed_up = lax.all_gather(after(expert_up, qkv_full), "fsdp", axis=1, tiled=True)[0]
    routed_down = lax.all_gather(after(expert_down, qkv_full), "fsdp", axis=1, tiled=True)[0]
    keys, values = keys_values[:, :HEAD_DIM], keys_values[:, HEAD_DIM:]
    query = (
        rotate(qkv[:, :heads_wide].reshape(group_rows, group, HEAD_DIM), cosine, sine_table)
        .astype(low)
        .reshape(group_rows, heads_wide)
    )
    probs, attended = run_attention(
        query, keys, values, group_pos[:, None], seq_pos[None, :]
    )
    shared_rows = deal_planes(after(shared_piece, kv_own))
    attended = after(attended, shared_rows)
    state_part = dot32("th,dh->td", attended, out_weight).astype(low)
    token_in = inputs[0].astype(jnp.float32)
    state = token_in + scatter_group(state_part.reshape(CORES, LINES, tok_rows, width))

    inverse_two = lax.rsqrt(jnp.mean(state * state, axis=-1, keepdims=True) + epsilon)
    normed_two = state * inverse_two
    moe_in = (normed_two * gain_two).astype(low)
    if lax.axis_size("fsdp") == 2:
        shared_peer = swap(after(shared_rows, attended))
    moe_lines = plane_lines(moe_in)
    all_moe = gather_ctx(moe_lines)
    cot_lines = plane_lines(after(cotangent[0], keys_values))
    all_cot = gather_ctx({k: after(line, moe_in) for k, line in cot_lines.items()})
    if lax.axis_size("fsdp") == 2:
        shared_peer = after(shared_peer, moe_lines[plane_order()[-1]])
        first = lax.axis_index("fsdp") == 0
        shared_weight = jnp.concatenate(
            [
                jnp.where(first, shared_rows, shared_peer),
                jnp.where(first, shared_peer, shared_rows),
            ],
            axis=2,
        ).reshape(width, -1)
    else:
        shared_weight = gather_fsdp(shared_rows, 2).reshape(width, -1)
    shared_parts = [
        shared_weight[:, at * hidden_part : (at + 1) * hidden_part] for at in range(3)
    ]
    (
        moe_keep,
        moe_near,
        out_keep,
        out_near,
        received,
        slot_grad,
        expert_hidden,
        grad_expert_a,
        grad_expert_b,
        shared_hidden,
        grad_shared_a,
        grad_shared_b,
        gates,
    ) = run_experts(
        all_moe,
        all_cot,
        named,
        place,
        place_t,
        own_expert,
        router_wide,
        [gate_first, gate_second, routed_up, routed_down],
        shared_parts,
    )

    sent = {}

    grad_down = outer(expert_hidden, slot_grad)
    sent["down"] = send_fsdp(grad_down, 0)
    moe_keep = after(moe_keep, grad_down)

    def first_work(values):
        held = after(received, *values)
        rows = after(all_moe, *values)
        return outer(held, grad_expert_a), outer(rows, grad_shared_a)

    def second_work(values):
        up = outer(after(received, *values), grad_expert_b)
        sent["gate"] = send_fsdp(works_done[0], 0, sent["down"][1], up)
        sent["up"] = send_fsdp(up, 0, sent["gate"][1])
        return up, sent["gate"][2]

    def third_work(values):
        rows = after(all_moe, *values)
        grad_shared = jnp.concatenate(
            [
                after(works_done[1], *values),
                outer(rows, grad_shared_b),
                outer(after(all_cot, *values), shared_hidden),
            ],
            axis=1,
        )
        sent["shared"] = send_fsdp(
            grad_shared.reshape(ctx_count, -1, 3 * hidden_part), 1, sent["up"][1]
        )
        return (grad_shared,)

    works_done = {}

    def keep_first(values):
        done = first_work(values)
        works_done[0], works_done[1] = done
        return done

    moe_sum, weight_grads, out_rows = scatter_two(
        (moe_keep, moe_near),
        (out_keep, out_near),
        [keep_first, second_work, third_work],
        lambda: [sent["gate"][1]],
    )
    out_steps = out_rows(moe_sum)
    out_moved = [next(out_steps)]
    for unused in plane_order()[1:]:
        out_moved.append(out_steps.send(moe_sum))
    grad_moe_sum = moe_sum[:, :width]
    grad_gates = moe_sum[:, width : width + experts].T

    home_gates = gates[:tok_rows, :experts].T
    gate_mean = jnp.sum(home_gates * grad_gates, axis=0, keepdims=True)
    grad_logits = home_gates * (grad_gates - gate_mean)
    grad_router = jnp.einsum(
        "td,et->de", moe_in.astype(jnp.float32), grad_logits, precision=highest
    )
    grad_moe_in = grad_moe_sum + jnp.einsum(
        "et,de->td", grad_logits, router_weight.astype(jnp.float32), precision=highest
    )
    grad_gain_two, grad_through = norm_back(grad_moe_in, normed_two, inverse_two, gain_two)
    grad_state = cotangent[0].astype(jnp.float32) + grad_through
    group_proj = gather_group(grad_state.astype(low)).reshape(group_rows, width)
    grad_expert_down = add_fsdp(*sent["down"])
    group_proj, grad_expert_down = together(group_proj, grad_expert_down)

    grad_attended = dot32("td,dh->th", group_proj, out_weight).astype(low)
    grad_query_rot, grad_kv_part = run_attention_back(probs, grad_attended, query, keys, values)
    grad_query_rot = grad_query_rot.reshape(group_rows, group, HEAD_DIM)
    grad_expert_gate = add_fsdp(*sent["gate"])
    grad_kv_part, *unused = together(grad_kv_part, *out_moved)
    up_arrived = sent["up"][1]
    grad_kv_part = grad_kv_part.reshape(plane_count(), group_rows, 2 * HEAD_DIM)
    kv_away = planes_away(grad_kv_part)
    grad_keys_values = scatter_planes(grad_kv_part, away=kv_away)
    grad_expert_up = add_fsdp(sent["up"][0], up_arrived)
    grad_query_pre = (
        rotate(grad_query_rot, cosine, -sine_table).astype(low).reshape(group_rows, heads_wide)
    )
    query_sent = send_grads(
        dot32("td,th->dh", attn_in, grad_query_pre), sent["shared"][1]
    )
    grad_keys_values, grad_expert_gate, *unused = together(
        grad_keys_values, grad_expert_gate, sent["up"][1]
    )
    grad_keys_pre = rotate(grad_keys_values[:, None, :HEAD_DIM], cosine, -sine_table)[:, 0]
    grad_kv_pre = jnp.concatenate(
        [grad_keys_pre.astype(low), grad_keys_values[:, HEAD_DIM:].astype(low)], axis=1
    )
    attn_part = dot32("th,dh->td", grad_query_pre, qkv_weight[:, :heads_wide]) + dot32(
        "th,dh->td", grad_kv_pre, qkv_weight[:, heads_wide:]
    )
    grad_attn_in = scatter_group(attn_part.astype(low).reshape(CORES, LINES, tok_rows, width))
    grad_gain_one = jnp.sum(attn_part * normed_in, axis=0)
    grad_kv = jnp.concatenate(
        [
            dot32("td,th->dh", attn_in, grad_kv_pre),
            grad_gain_one[:, None],
            grad_gain_two[:, None],
            jnp.pad(grad_router, ((0, 0), (0, HEAD_DIM - 2 - experts))),
        ],
        axis=1,
    )
    shared_back = collected(*sent["shared"][:2], low)
    grad_attn_in, query_arrived = together(grad_attn_in, query_sent[1])
    grad_kv = after(grad_kv, grad_attn_in)
    kv_sent = send_grads(grad_kv, query_arrived)
    query_planes = scatter_planes(
        plane_view(add_fsdp(query_sent[0], after(query_arrived, kv_sent[2])))
    )
    back_gate = shared_back[:, :, :hidden_part].reshape(part_rows, -1)
    back_up = shared_back[:, :, hidden_part : 2 * hidden_part].reshape(part_rows, -1)
    back_down = shared_back[:, :, 2 * hidden_part :].reshape(part_rows, -1).T
    output = (state + out_steps.send(grad_keys_values)).astype(low)
    kv_arrived = after(kv_sent[1], back_gate, back_up, back_down, output, grad_expert_up)
    kv_total = plane_view(add_fsdp(kv_sent[0], kv_arrived))
    out_own, out_arrived = planes_sent(
        grads_view(dot32("td,th->dh", group_proj, after(attended, *kv_away.values())))
    )
    kv_total, out_own = together(kv_total, out_own)
    kv_planes = scatter_planes(kv_total)
    out_planes = planes_total(out_own, out_arrived)
    planes_sum = jnp.concatenate(
        [query_planes, scatter_fsdp(out_planes, 1)[:, 0], kv_planes], axis=2
    )
    planes_sum, grad_attn_in, back_gate, back_up, back_down, output = together(
        planes_sum, grad_attn_in, back_gate, back_up, back_down, output
    )
    all_back = undeal_group(
        planes_sum.astype(low).reshape(LINES, CORES, part_rows, planes_sum.shape[2])
    )
    all_back = all_back.reshape(part_rows, CHIP, -1).astype(jnp.float32)
    query_back = all_back[:, :, :heads_wide]
    out_back = all_back[:, :, heads_wide : 2 * heads_wide]
    kv_back = all_back[:, :, 2 * heads_wide :]
    narrow_back = jnp.sum(kv_back[:, :, 2 * HEAD_DIM :], axis=1)
    home_inverse = lax.rsqrt(jnp.mean(token_in * token_in, axis=-1, keepdims=True) + epsilon)
    unused, grad_first = norm_back(grad_attn_in, token_in * home_inverse, home_inverse, gain_one)
    grad_inputs = (grad_state + grad_first).astype(low)

    return (
        output[None],
        grad_inputs[None],
        narrow_back[:, 0],
        query_back.reshape(part_rows, -1),
        kv_back[:, :, :HEAD_DIM].reshape(part_rows, -1),
        kv_back[:, :, HEAD_DIM : 2 * HEAD_DIM].reshape(part_rows, -1),
        out_back.reshape(part_rows, -1).T,
        narrow_back[:, 1],
        narrow_back[:, 2 : 2 + experts],
        back_gate,
        back_up,
        back_down,
        grad_expert_gate[None],
        grad_expert_up[None],
        grad_expert_down[None],
    )


def solution(mesh):
    in_specs = (
        P("fsdp", "ctx", None),
        P(("ctx", "fsdp")),
        P(("ctx", "fsdp"), None),
        P(("ctx", "fsdp"), None),
        P(("ctx", "fsdp"), None),
        P(None, ("ctx", "fsdp")),
        P(("ctx", "fsdp")),
        P(("ctx", "fsdp"), None),
        P(("ctx", "fsdp"), None),
        P(("ctx", "fsdp"), None),
        P(None, ("ctx", "fsdp")),
        P("ctx", "fsdp", None),
        P("ctx", "fsdp", None),
        P("ctx", "fsdp", None),
        P("fsdp", None),
        P("fsdp", "ctx", None),
        P("fsdp", "ctx", None),
    )
    out_specs = (
        P("fsdp", "ctx", None),
        P("fsdp", "ctx", None),
        P(("ctx", "fsdp")),
        P(("ctx", "fsdp"), None),
        P(("ctx", "fsdp"), None),
        P(("ctx", "fsdp"), None),
        P(None, ("ctx", "fsdp")),
        P(("ctx", "fsdp")),
        P(("ctx", "fsdp"), None),
        P(("ctx", "fsdp"), None),
        P(("ctx", "fsdp"), None),
        P(None, ("ctx", "fsdp")),
        P("ctx", "fsdp", None),
        P("ctx", "fsdp", None),
        P("ctx", "fsdp", None),
    )
    return jax.shard_map(body, mesh=mesh, in_specs=in_specs, out_specs=out_specs, check_vma=False)
```
